32 devices in a mesh: group: 8 (over z, y), row: 4 (over x, core).
Axes of the slice: x: 2, y: 2, z: 4, core: 2. Of those that a mesh axis runs over, the one named last changes fastest.
Arguments:
- frames: bfloat16 [48, 16, 32, 384], P('group', 'row'), may hold values from -30 to 30
- clip_lengths: int32 [3], replicated, may hold values from 2 to 11, as said below
- group_start: int32 [8], P('group'), may hold values from 0 to 22, as said below
- group_count: int32 [8], P('group'), may hold values from 2 to 6, as said below
- kernel_one: bfloat16 [3, 3, 3, 384, 384], P(None, None, None, 'group'), may hold values from -0.0625 to 0.0625
- kernel_two: bfloat16 [3, 3, 3, 384, 384], P(None, None, None, 'group'), may hold values from -0.0625 to 0.0625
- gain_one: float32 [384], replicated, may hold values from 0.1 to 1.9
- gain_two: float32 [384], replicated, may hold values from 0.1 to 1.9
Outputs:
- decoded: bfloat16 [48, 16, 32, 384], P('group', 'row')
The draws below stay inside these ranges and needn't reach their ends.
Inputs may be any that keep to these rules, and one draw needn't show every extreme that they name: group_start is the exclusive prefix sum of group_count over the devices. `group_count`: a quarter of the devices, never the last one, hold 6 frames, the others 2; the counts sum to 24. `clip_lengths`: one clip has exactly 11 frames; the three sum to 24.
All inputs are finite; a program needn't handle non-finite values.
Results may differ from the reference program's by a relative error of at most 0.0029.
Values may be sent and summed in bfloat16 or wider, within the bound.
A program may use at most 128 MiB of HBM per device.

```python
import math
import jax
import jax.numpy as jnp
from jax import lax

C = 384
COLS = 32
CAP = 6
H = 16
SLOTS = 48
TOTAL_FRAMES = 24
CLIP_MOST = 11
N_GROUP = 8


def group_layout(key):
    order = jax.random.permutation(key, N_GROUP - 1)
    pattern = jnp.where(jnp.arange(N_GROUP - 1) < N_GROUP // 4, CAP, 2).astype(jnp.int32)
    counts = jnp.concatenate([jnp.take(pattern, order), jnp.full((1,), 2, jnp.int32)]).astype(jnp.int32)
    starts = (jnp.cumsum(counts) - counts).astype(jnp.int32)
    return (counts, starts)


def draw_group_count(key, part):
    return group_layout(key)[0]


def draw_group_start(key, part):
    return group_layout(key)[1]


def draw_clip_lengths(key, part):
    key = jax.random.fold_in(key, 13)
    pick_key, order_key = jax.random.split(key)
    remain = TOTAL_FRAMES - CLIP_MOST
    first = jax.random.randint(pick_key, (), remain - CLIP_MOST, CLIP_MOST + 1).astype(jnp.int32)
    lengths = jnp.stack([jnp.full((), CLIP_MOST, jnp.int32), first, (remain - first).astype(jnp.int32)])
    order = jax.random.permutation(order_key, 3)
    return jnp.take(lengths, order).astype(jnp.int32)


def draw_frames(key, part):
    key = jax.random.fold_in(key, 7)
    base_key, rough_key, channel_key = jax.random.split(key, 3)
    dims = (SLOTS, H, COLS, C)
    row_pos = jnp.arange(H).astype(jnp.float32) / (H - 1)
    rising = jnp.exp(row_pos * math.log(3.0))
    roughness = jnp.exp(jax.random.uniform(rough_key, (SLOTS, H, 1, 1), jnp.float32, 0.0, math.log(3.2)))
    channel_scale = jnp.exp(jax.random.uniform(channel_key, (C,), jnp.float32, math.log(0.1), 0.0))
    base = jnp.clip(jax.random.normal(base_key, dims, jnp.float32), -3.0, 3.0)
    values = base * rising[None, :, None, None] * roughness * channel_scale
    return values.astype(jnp.bfloat16)


def levels(own_key, shape, pieces, smallest, largest):
    loudness = 1.0
    for dim, parts in pieces:
        heights = jax.random.uniform(jax.random.fold_in(jax.random.fold_in(own_key, 6), dim), (parts,), jnp.float32, smallest / len(pieces), largest / len(pieces))
        loudness = loudness * jnp.repeat(jnp.exp(heights), shape[dim] // parts).reshape((-1,) + (1,) * (len(shape) - 1 - dim))
    return loudness


def scatter_about(key, shape, width, most, pieces=(), held_as=jnp.bfloat16):
    drawn = width * jax.random.normal(key, shape, jnp.float32)
    if pieces:
        drawn = drawn * levels(key, shape, pieces, -0.22, 0.18)
    return jnp.clip(drawn, -most, most).astype(held_as)


def setup_inputs(seed: int = 0) -> dict:
    keys = jax.random.split(jax.random.key(seed), 9)
    return {
        "frames": draw_frames(jax.random.fold_in(keys[8], 71), 0),
        "clip_lengths": draw_clip_lengths(jax.random.fold_in(keys[8], 71), 0),
        "group_start": draw_group_start(jax.random.fold_in(keys[8], 71), 0),
        "group_count": draw_group_count(jax.random.fold_in(keys[8], 71), 0),
        "kernel_one": scatter_about(keys[4], (3, 3, 3, C, C), (27 * C) ** -0.5, 0.0625, ((3, 8),)),
        "kernel_two": scatter_about(keys[5], (3, 3, 3, C, C), (27 * C) ** -0.5, 0.0625, ((3, 8),)),
        "gain_one": jnp.clip(1.0 + 0.18 * jax.random.normal(keys[6], (C,), jnp.float32), 0.1, 1.9),
        "gain_two": jnp.clip(1.0 + 0.18 * jax.random.normal(keys[7], (C,), jnp.float32), 0.1, 1.9),
    }


def norm_act(values, gain):
    data = values.astype(jnp.float32)
    mean_square = lax.optimization_barrier(jnp.mean(data * data, axis=-1, keepdims=True))
    scaled = data * lax.rsqrt(mean_square + 1e-06)
    return jax.nn.silu(scaled * gain).astype(jnp.bfloat16)

def causal_conv(acts, kernel, position):
    data = acts.astype(jnp.float32)
    frames_n = data.shape[0]
    summed = jnp.zeros(data.shape, jnp.float32)
    for lag_index in range(3):
        lag = 2 - lag_index
        if lag > 0:
            shifted = jnp.concatenate([jnp.zeros((lag,) + data.shape[1:], jnp.float32), data[:frames_n - lag]], 0)
        else:
            shifted = data
        contrib = lax.conv_general_dilated(shifted, kernel[lag_index].astype(jnp.float32), (1, 1), ((1, 1), (1, 1)), dimension_numbers=('NHWC', 'HWIO', 'NHWC'))
        keep_frame = (position >= lag).astype(jnp.float32)
        summed = summed + keep_frame[:, None, None, None] * contrib
    return summed

def reference(frames, clip_lengths, group_start, group_count, kernel_one, kernel_two, gain_one, gain_two):
    frame_index = jnp.arange(TOTAL_FRAMES, dtype=jnp.int32)
    owner = lax.optimization_barrier(jnp.sum((group_start[None, :] <= frame_index[:, None]).astype(jnp.int32), axis=1)) - 1
    slot_ids = (owner * CAP + frame_index - jnp.take(group_start, owner)).astype(jnp.int32)
    seq = jnp.take(frames, slot_ids, axis=0)
    ends = jnp.cumsum(clip_lengths).astype(jnp.int32)
    begins = lax.optimization_barrier(jnp.max(jnp.where(ends[None, :] <= frame_index[:, None], ends[None, :], 0), axis=1)).astype(jnp.int32)
    position = frame_index - begins
    act_one = norm_act(seq, gain_one)
    middle = causal_conv(act_one, kernel_one, position)
    act_two = norm_act(middle, gain_two)
    result = seq.astype(jnp.float32) + causal_conv(act_two, kernel_two, position)
    slot_all = jnp.arange(SLOTS, dtype=jnp.int32)
    device_of = (slot_all // CAP).astype(jnp.int32)
    within = slot_all - device_of * CAP
    live_slot = within < jnp.take(group_count, device_of)
    source = jnp.minimum(jnp.take(group_start, device_of) + within, TOTAL_FRAMES - 1).astype(jnp.int32)
    picked = jnp.take(result, source, axis=0)
    return jnp.where(live_slot[:, None, None, None], picked, 0.0).astype(jnp.bfloat16)
```

```python
import functools
import math

import jax
import jax.numpy as jnp
from jax import lax
from jax.experimental import pallas as pl
from jax.experimental.pallas import tpu as pltpu
from jax.sharding import PartitionSpec as P

MESH = pl.DeviceIdType.MESH
BF16 = jnp.bfloat16
F32 = jnp.float32


def clip_positions(clip_lengths, frame_index):
    ends = jnp.cumsum(clip_lengths)
    begins = jnp.max(jnp.where(ends[None, :] <= frame_index[:, None], ends[None, :], 0), axis=1)
    return frame_index - begins


def norm_act(data, gain):
    mean_square = jnp.mean(data * data, axis=-1, keepdims=True)
    scaled = data * lax.rsqrt(mean_square + 1e-06) * gain
    return (scaled / (1.0 + jnp.exp(-scaled))).astype(BF16)


def kernel(
    layout, gathers,
    frames, k1, k2, gain1, gain2, masks, live, count,
    out,
    w1, w2, act, last, pad, a3, acc,
    piece_recv, piece_send, halo_recv, halo_send, own_sem,
):
    nz, ny, nr = layout
    ng = nz * ny
    slots, rows, cols, ch = frames.shape
    per = rows * cols
    g, r = lax.axis_index("group"), lax.axis_index("row")
    z, y = g // ny, g % ny
    x, c = r // 2, r % 2
    weights = (w1, w2)
    kernels = (k1, k2)
    pending = []

    always = g >= 0
    up = (z < nz - 1, g + ny, r)
    down = (z > 0, g - ny, r)
    across = (always, z * ny + (1 - y), r)
    sibling = (always, g, x * 2 + (1 - c))
    other = (always, g, (1 - x) * 2 + (1 - c))

    greet = []
    if gathers:
        greet += [up, down, across, sibling, other]
    for dr in (-1, 0, 1):
        ok_r = jnp.logical_and(r + dr >= 0, r + dr < nr)
        for dg in (-1, 0, 1):
            if dr == 0 and dg == 0:
                continue
            ok = jnp.logical_and(ok_r, jnp.logical_and(g + dg >= 0, g + dg < ng))
            greet.append((ok, g + dg, r + dr))
    barrier = pltpu.get_barrier_semaphore()
    total = 0
    for ok, tg, tr in greet:
        @pl.when(ok)
        def _(tg=tg, tr=tr):
            pl.semaphore_signal(barrier, inc=1, device_id=(tg, tr), device_id_type=MESH)
        total = total + ok.astype(jnp.int32)
    pl.semaphore_wait(barrier, total)

    def send(ok, src, dst, ssem, rsem, tg, tr):
        copy = pltpu.make_async_remote_copy(
            src_ref=src, dst_ref=dst, send_sem=ssem, recv_sem=rsem,
            device_id=(tg, tr), device_id_type=MESH,
        )

        @pl.when(ok)
        def _():
            copy.start()
        pending.append((ok, copy))

    if gathers:
        depth = k1.shape[3]
        mine = 2 * c + (1 - c) * x

        def piece(i, t, s):
            return weights[i].at[t, :, :, pl.ds(pl.multiple_of(s * depth, depth), depth), :]

        def send_piece(i, t, s, way, ok, to, src=None):
            there = piece(i, t, s)
            send(
                ok, there if src is None else src, there,
                piece_send.at[i, s, way], piece_recv.at[i, t, s], to[1], to[2],
            )

        def wait_piece(i, t, s, ok):
            there = piece(i, t, s)

            @pl.when(ok)
            def _():
                pltpu.make_async_remote_copy(
                    src_ref=there, dst_ref=there, send_sem=piece_send.at[i, s, 0],
                    recv_sem=piece_recv.at[i, t, s], device_id=(g, sibling[2]),
                    device_id_type=MESH,
                ).wait_recv()

        def land_own(i):
            return pltpu.make_async_copy(
                kernels[i],
                weights[i].at[:, :, :, pl.ds(pl.multiple_of(g * depth, depth), depth), :],
                own_sem.at[i],
            )

        def start_own(i):
            src = kernels[i].at[mine]
            send_piece(i, mine, g, 0, up[0], up, src)
            send_piece(i, mine, g, 1, down[0], down, src)
            send_piece(i, mine, g, 2, always, across, src)

        def both(a, b):
            return jnp.logical_and(a, b)

        def arrivals(step):
            kind, d = step
            row_y = y if kind == "z" else 1 - y
            found = []
            for sign in ((-1, 1) if d else (1,)):
                zz = z + sign * d
                ok = both(zz >= 0, zz < nz)
                s = jnp.clip(zz, 0, nz - 1) * ny + row_y
                found.append((ok, s, sign))
            return found

        steps = [("z", 1), ("y", 0)]
        for d in range(2, nz):
            steps += [("z", d), ("y", d - 1)]
        steps += [("y", nz - 1)]

        def relay(i, step):
            for ok, s, sign in arrivals(step):
                wait_piece(i, mine, s, ok)
                if step[0] == "z":
                    if sign < 0:
                        send_piece(i, mine, s, 0, both(ok, up[0]), up)
                    else:
                        send_piece(i, mine, s, 1, both(ok, down[0]), down)
                    send_piece(i, mine, s, 2, ok, across)
                send_piece(i, mine, s, 3, both(ok, c == 0), other)
                send_piece(i, mine, s, 4, ok, sibling)

        def relay_crossed(i, step):
            for ok, s, _ in arrivals(step):
                here = both(ok, c == 1)
                wait_piece(i, 1 - x, s, here)
                send_piece(i, 1 - x, s, 5, here, sibling)

        def full(i, n):
            relay(i, steps[n])
            if n:
                relay_crossed(i, steps[n - 1])

        def finish(i):
            relay_crossed(i, steps[-1])
            for step in steps:
                for ok, s, _ in arrivals(step):
                    wait_piece(i, 2 * (1 - c) + c * x, s, ok)
                    wait_piece(i, 1 - x, s, both(ok, c == 0))
            land_own(i).wait()

        land_own(0).start()
        land_own(1).start()
        start_own(0)

    def share_edges(i, read, gain):
        for s in range(slots):
            done = norm_act(read(s), gain[...]).reshape(rows, cols, ch)
            act[i, s] = done
            pad[i, 2 + s, 1 : 1 + rows] = done
        last[i] = act[i, pl.ds(jnp.clip(count[0] - 2, 0, slots - 2), 2)]

        @pl.when(r == 0)
        def _():
            pad[i, :, 0] = jnp.zeros((slots + 2, cols, ch), BF16)

        @pl.when(r == nr - 1)
        def _():
            pad[i, :, rows + 1] = jnp.zeros((slots + 2, cols, ch), BF16)

        @pl.when(g == 0)
        def _():
            pad[i, 0:2] = jnp.zeros((2, rows + 2, cols, ch), BF16)

        mine_in = pad.at[i]
        below, above, after = r < nr - 1, r > 0, g < ng - 1
        whole = pl.ds(2, slots)
        two = pl.ds(0, 2)
        plan = [
            (below, act.at[i, :, rows - 1], mine_in.at[whole, 0], g, r + 1, r > 0),
            (above, act.at[i, :, 0], mine_in.at[whole, rows + 1], g, r - 1, r < nr - 1),
            (after, last.at[i], mine_in.at[two, pl.ds(1, rows)], g + 1, r, g > 0),
            (
                jnp.logical_and(after, below), last.at[i, :, rows - 1],
                mine_in.at[two, 0], g + 1, r + 1, jnp.logical_and(g > 0, r > 0),
            ),
            (
                jnp.logical_and(after, above), last.at[i, :, 0],
                mine_in.at[two, rows + 1], g + 1, r - 1, jnp.logical_and(g > 0, r < nr - 1),
            ),
        ]
        waits = []
        for n, (ok, src, dst, tg, tr, comes) in enumerate(plan):
            send(ok, src, dst, halo_send.at[i, n], halo_recv.at[i, n], tg, tr)
            waits.append((comes, pending[-1][1]))
        return waits

    def gather_columns(i, waits):
        for comes, copy in waits:
            @pl.when(comes)
            def _(copy=copy):
                copy.wait_recv()
        size = (rows + 2) * cols
        col = lax.broadcasted_iota(jnp.int32, (size, ch), 0) % cols

        def body(f, carry):
            middle = pad[i, f].reshape(size, ch)
            wide = middle.astype(F32)
            left = jnp.where(col == 0, 0.0, pltpu.roll(wide, 1, 0)).astype(BF16)
            right = jnp.where(col == cols - 1, 0.0, pltpu.roll(wide, size - 1, 0)).astype(BF16)
            shape = (rows + 2, cols, ch)
            a3[f, :, :, 0:ch] = left.reshape(shape)
            a3[f, :, :, ch : 2 * ch] = middle.reshape(shape)
            a3[f, :, :, 2 * ch : 3 * ch] = right.reshape(shape)
            return carry

        lax.fori_loop(0, slots + 2, body, 0)

    def clear():
        acc[...] = jnp.zeros(acc.shape, F32)

    def taps(i, t):
        def body(p, carry):
            lhs = a3[pl.ds(t, slots), pl.ds(p, rows)].reshape(slots * per, 3 * ch)
            rhs = weights[i][t, p].reshape(3 * ch, ch)
            part = jnp.dot(lhs, rhs, preferred_element_type=F32)
            for s in range(slots):
                acc[s] += part[s * per : (s + 1) * per] * masks[t * slots + s]
            return carry

        lax.fori_loop(0, 3, body, 0)

    if not gathers:
        weights = (k1, k2)
    waits = share_edges(0, lambda s: frames[s].reshape(per, ch).astype(F32), gain1)
    if gathers:
        full(0, 0)
    gather_columns(0, waits)
    clear()
    if gathers:
        for n in range(1, len(steps)):
            full(0, n)
            if n == 3:
                start_own(1)
        full(1, 0)
        finish(0)
    for t in range(3):
        taps(0, t)
        if gathers:
            full(1, t + 1)
    waits = share_edges(1, lambda s: acc[s], gain2)
    if gathers:
        full(1, 4)
    gather_columns(1, waits)
    clear()
    if gathers:
        for n in range(5, len(steps)):
            full(1, n)
        finish(1)

    def second(t, carry):
        taps(1, t)
        return carry

    lax.fori_loop(0, 3, second, 0)
    for s in range(slots):
        summed = frames[s].reshape(per, ch).astype(F32) + acc[s]
        kept = jnp.where(jnp.full(summed.shape, live[s], F32) > 0.0, summed, 0.0)
        out[s] = kept.astype(BF16).reshape(rows, cols, ch)
    for ok, copy in pending:
        @pl.when(ok)
        def _(copy=copy):
            copy.wait_send()


def per_device(
    layout, frames, clip_lengths, group_start, group_count, kernel_one, kernel_two, gain_one, gain_two
):
    nz, ny, nr = layout
    slots, rows, cols, ch = frames.shape
    depth = kernel_one.shape[3]
    gathers = depth % 16 == 0 and ny == 2 and nr == 4
    position = clip_positions(clip_lengths, group_start[0] + jnp.arange(slots, dtype=jnp.int32))
    masks = (position[None, :] >= jnp.array([2, 1, 0])[:, None]).astype(F32).reshape(-1)
    live = (jnp.arange(slots, dtype=jnp.int32) < group_count[0]).astype(F32)
    if not gathers:
        kernel_one = lax.all_gather(kernel_one, "group", axis=3, tiled=True)
        kernel_two = lax.all_gather(kernel_two, "group", axis=3, tiled=True)
    vmem = pl.BlockSpec(memory_space=pltpu.VMEM)
    smem = pl.BlockSpec(memory_space=pltpu.SMEM)
    weight_spec = pl.BlockSpec(memory_space=pl.ANY) if gathers else vmem
    full = (3, 3, 3, ch, ch) if gathers else (8, 128)
    shards = lax.axis_size("group")
    dma = pltpu.SemaphoreType.DMA
    return pl.pallas_call(
        functools.partial(kernel, layout, gathers),
        out_shape=jax.ShapeDtypeStruct(frames.shape, BF16),
        in_specs=[vmem, weight_spec, weight_spec, vmem, vmem, smem, smem, smem],
        out_specs=vmem,
        scratch_shapes=[
            pltpu.VMEM(full, BF16),
            pltpu.VMEM(full, BF16),
            pltpu.VMEM((2, slots, rows, cols, ch), BF16),
            pltpu.VMEM((2, 2, rows, cols, ch), BF16),
            pltpu.VMEM((2, slots + 2, rows + 2, cols, ch), BF16),
            pltpu.VMEM((slots + 2, rows + 2, cols, 3 * ch), BF16),
            pltpu.VMEM((slots, rows * cols, ch), F32),
            dma((2, 3, shards) if gathers else (1,)),
            dma((2, shards, 6) if gathers else (1,)),
            dma((2, 5)),
            dma((2, 5)),
            dma((2,)),
        ],
        compiler_params=pltpu.CompilerParams(
            collective_id=0, has_side_effects=True, vmem_limit_bytes=56 * 1024 * 1024
        ),
    )(
        frames, kernel_one, kernel_two, gain_one[None, :], gain_two[None, :], masks, live, group_count
    )


def solution(mesh):
    groups, rows = mesh.shape["group"], mesh.shape["row"]
    ny = math.isqrt(groups // 2)
    return jax.shard_map(
        functools.partial(per_device, (groups // ny, ny, rows)),
        mesh=mesh,
        in_specs=(
            P("group", "row", None, None),
            P(),
            P("group"),
            P("group"),
            P(None, None, None, "group", None),
            P(None, None, None, "group", None),
            P(),
            P(),
        ),
        out_specs=P("group", "row", None, None),
        check_vma=False,
    )
```

```python
import functools
import math

import jax
import jax.numpy as jnp
from jax import lax
from jax.experimental import pallas as pl
from jax.experimental.pallas import tpu as pltpu
from jax.sharding import PartitionSpec as P

MESH = pl.DeviceIdType.MESH
BF16 = jnp.bfloat16
F32 = jnp.float32


def norm_act(data, gain):
    mean_square = jnp.mean(data * data, axis=-1, keepdims=True)
    scaled = data * lax.rsqrt(mean_square + 1e-06) * gain
    return (scaled / (1.0 + jnp.exp(-scaled))).astype(BF16)


def kernel(
    layout, gathers,
    frames, k1, k2, gain1, gain2, lengths, start, count,
    out,
    w, act, last, pad, a3, acc,
    piece_recv, piece_send, halo_recv, halo_send, own_sem,
):
    nz, ny, nr = layout
    ng = nz * ny
    slots, rows, cols, ch = frames.shape
    per = rows * cols
    g, r = lax.axis_index("group"), lax.axis_index("row")
    z, y = g // ny, g % ny
    x, c = r // 2, r % 2
    kernels = (k1, k2)
    pending = []

    always = g >= 0
    up = (z < nz - 1, g + ny, r)
    down = (z > 0, g - ny, r)
    across = (always, z * ny + (1 - y), r)
    sibling = (always, g, x * 2 + (1 - c))
    other = (always, g, (1 - x) * 2 + (1 - c))

    greet = []
    if gathers:
        greet += [up, down, across, sibling, other]
    for dr in (-1, 0, 1):
        ok_r = jnp.logical_and(r + dr >= 0, r + dr < nr)
        for dg in (-1, 0, 1):
            if dr == 0 and dg == 0:
                continue
            ok = jnp.logical_and(ok_r, jnp.logical_and(g + dg >= 0, g + dg < ng))
            greet.append((ok, g + dg, r + dr))
    if gathers:
        depth = k1.shape[3]
        own = pl.ds(pl.multiple_of(g * depth, depth), depth)
        landings = [
            pltpu.make_async_copy(
                kernels[n // 3].at[:, n % 3], w.at[n, :, :, own, :], own_sem.at[n]
            )
            for n in range(6)
        ]
        for landing in landings:
            landing.start()
    barrier = pltpu.get_barrier_semaphore()
    total = 0
    for ok, tg, tr in greet:
        @pl.when(ok)
        def _(tg=tg, tr=tr):
            pl.semaphore_signal(barrier, inc=1, device_id=(tg, tr), device_id_type=MESH)
        total = total + ok.astype(jnp.int32)
    pl.semaphore_wait(barrier, total)

    def send(ok, src, dst, ssem, rsem, tg, tr):
        copy = pltpu.make_async_remote_copy(
            src_ref=src, dst_ref=dst, send_sem=ssem, recv_sem=rsem,
            device_id=(tg, tr), device_id_type=MESH,
        )

        @pl.when(ok)
        def _():
            copy.start()
        pending.append((ok, copy))

    if gathers:
        mine = 2 * c + (1 - c) * x

        def piece(n, t, s):
            return w.at[n, t, :, pl.ds(pl.multiple_of(s * depth, depth), depth), :]

        def piece_copy(n, t, s, way, to):
            there = piece(n, t, s)
            return pltpu.make_async_remote_copy(
                src_ref=there, dst_ref=there, send_sem=piece_send.at[n, s, way],
                recv_sem=piece_recv.at[n, t, s], device_id=(to[1], to[2]),
                device_id_type=MESH,
            )

        def send_piece(n, t, s, way, ok, to):
            @pl.when(ok)
            def _():
                piece_copy(n, t, s, way, to).start()

        def sent_piece(n, t, s, way, ok, to):
            @pl.when(ok)
            def _():
                piece_copy(n, t, s, way, to).wait_send()

        def wait_piece(n, t, s, ok):
            @pl.when(ok)
            def _():
                piece_copy(n, t, s, 0, sibling).wait_recv()

        def both(a, b):
            return jnp.logical_and(a, b)

        def own_pieces(n, act_on):
            act_on(n, mine, g, 0, up[0], up)
            act_on(n, mine, g, 1, down[0], down)
            act_on(n, mine, g, 2, always, across)

        def arrivals(step):
            kind, d = step
            row_y = y if kind == "z" else 1 - y
            found = []
            for sign in ((-1, 1) if d else (1,)):
                zz = z + sign * d
                ok = both(zz >= 0, zz < nz)
                s = jnp.clip(zz, 0, nz - 1) * ny + row_y
                found.append((ok, s, sign))
            return found

        steps = [("z", 1), ("y", 0)]
        for d in range(2, nz):
            steps += [("z", d), ("y", d - 1)]
        steps += [("y", nz - 1)]

        def passed_on(n, step, ok, s, sign, act_on):
            if step[0] == "z":
                if sign < 0:
                    act_on(n, mine, s, 0, both(ok, up[0]), up)
                else:
                    act_on(n, mine, s, 1, both(ok, down[0]), down)
                act_on(n, mine, s, 2, ok, across)
            act_on(n, mine, s, 3, both(ok, c == 0), other)
            act_on(n, mine, s, 4, ok, sibling)

        def relay(n, k):
            for ok, s, sign in arrivals(steps[k]):
                wait_piece(n, mine, s, ok)
                passed_on(n, steps[k], ok, s, sign, send_piece)

        def cross(n, k):
            for ok, s, _ in arrivals(steps[k]):
                here = both(ok, c == 1)
                wait_piece(n, 1 - x, s, here)
                send_piece(n, 1 - x, s, 5, here, sibling)

        def finish(n):
            for step in steps:
                for ok, s, _ in arrivals(step):
                    wait_piece(n, 2 * (1 - c) + c * x, s, ok)
                    wait_piece(n, 1 - x, s, both(ok, c == 0))

        def drain(n, carry):
            own_pieces(n, sent_piece)
            for step in steps:
                for ok, s, sign in arrivals(step):
                    passed_on(n, step, ok, s, sign, sent_piece)
                    sent_piece(n, 1 - x, s, 5, both(ok, c == 1), sibling)
            return carry

        for landing in landings:
            landing.wait()
        own_pieces(0, send_piece)

    def share_edges(i, read, gain):
        for s in range(slots):
            done = norm_act(read(s), gain[...][None, :]).reshape(rows, cols, ch)
            act[i, s] = done
            pad[i, 2 + s, 1 : 1 + rows] = done
        last[i] = act[i, pl.ds(jnp.clip(count[0] - 2, 0, slots - 2), 2)]

        @pl.when(r == 0)
        def _():
            pad[i, :, 0] = jnp.zeros((slots + 2, cols, ch), BF16)

        @pl.when(r == nr - 1)
        def _():
            pad[i, :, rows + 1] = jnp.zeros((slots + 2, cols, ch), BF16)

        @pl.when(g == 0)
        def _():
            pad[i, 0:2] = jnp.zeros((2, rows + 2, cols, ch), BF16)

        mine_in = pad.at[i]
        below, above, after = r < nr - 1, r > 0, g < ng - 1
        whole = pl.ds(2, slots)
        two = pl.ds(0, 2)
        plan = [
            (below, act.at[i, :, rows - 1], mine_in.at[whole, 0], g, r + 1, r > 0),
            (above, act.at[i, :, 0], mine_in.at[whole, rows + 1], g, r - 1, r < nr - 1),
            (after, last.at[i], mine_in.at[two, pl.ds(1, rows)], g + 1, r, g > 0),
            (
                jnp.logical_and(after, below), last.at[i, :, rows - 1],
                mine_in.at[two, 0], g + 1, r + 1, jnp.logical_and(g > 0, r > 0),
            ),
            (
                jnp.logical_and(after, above), last.at[i, :, 0],
                mine_in.at[two, rows + 1], g + 1, r - 1, jnp.logical_and(g > 0, r < nr - 1),
            ),
        ]
        waits = []
        for n, (ok, src, dst, tg, tr, comes) in enumerate(plan):
            send(ok, src, dst, halo_send.at[i, n], halo_recv.at[i, n], tg, tr)
            waits.append((comes, pending[-1][1]))
        return waits

    def gather_columns(i, waits):
        for comes, copy in waits:
            @pl.when(comes)
            def _(copy=copy):
                copy.wait_recv()
        size = (rows + 2) * cols
        col = lax.broadcasted_iota(jnp.int32, (size, ch), 0) % cols

        def body(f, carry):
            middle = pad[i, f].reshape(size, ch)
            wide = middle.astype(F32)
            left = jnp.where(col == 0, 0.0, pltpu.roll(wide, 1, 0)).astype(BF16)
            right = jnp.where(col == cols - 1, 0.0, pltpu.roll(wide, size - 1, 0)).astype(BF16)
            shape = (rows + 2, cols, ch)
            a3[f, :, :, 0:ch] = left.reshape(shape)
            a3[f, :, :, ch : 2 * ch] = middle.reshape(shape)
            a3[f, :, :, 2 * ch : 3 * ch] = right.reshape(shape)
            return carry

        lax.fori_loop(0, slots + 2, body, 0)

    def clear():
        acc[...] = jnp.zeros(acc.shape, F32)

    position = []
    for s in range(slots):
        frame = start[0] + s
        begin, end = jnp.int32(0), jnp.int32(0)
        for m in range(lengths.shape[0]):
            end = end + lengths[m]
            begin = jnp.where(end <= frame, jnp.maximum(begin, end), begin)
        position.append(frame - begin)

    def taps(i, p, t):
        lhs = a3[t : t + slots, pl.ds(p, rows)].reshape(slots * per, 3 * ch)
        held = w[3 * i + p, t] if gathers else kernels[i][t, p]
        part = jnp.dot(lhs, held.reshape(3 * ch, ch), preferred_element_type=F32)
        for s in range(slots):
            here = part[s * per : (s + 1) * per]
            if t < 2:
                here = here * jnp.where(position[s] >= 2 - t, 1.0, 0.0)
            acc[s] += here

    def read_frame(s):
        return frames[s].reshape(per, ch).astype(F32)

    def phase(i, n, carry=0):
        relay(n, 0)
        cross(n - 1, 5)
        relay(n, 1)
        cross(n - 1, 6)
        finish(n - 1)
        taps(i, n - 1 - 3 * i, 0)
        relay(n, 2)
        cross(n, 0)

        @pl.when(n < 5)
        def _():
            own_pieces(n + 1, send_piece)
        taps(i, n - 1 - 3 * i, 1)
        relay(n, 3)
        cross(n, 1)
        taps(i, n - 1 - 3 * i, 2)
        for k in range(4, 7):
            relay(n, k)
            cross(n, k - 2)
        return carry

    def all_taps(i):
        def body(p, carry):
            for t in range(3):
                taps(i, p, t)
            return carry

        lax.fori_loop(0, 3, body, 0)

    if gathers:
        waits = share_edges(0, read_frame, gain1)
        relay(0, 0)
        relay(0, 1)
        gather_columns(0, waits)
        clear()
        relay(0, 2)
        cross(0, 0)
        own_pieces(1, send_piece)
        for k in range(3, 7):
            relay(0, k)
            cross(0, k - 2)
        lax.fori_loop(1, 3, functools.partial(phase_of, phase, 0), 0)
        relay(3, 0)
        cross(2, 5)
        relay(3, 1)
        cross(2, 6)
        finish(2)
        for t in range(3):
            taps(0, 2, t)
        relay(3, 2)
        cross(3, 0)
        own_pieces(4, send_piece)
        waits = share_edges(1, lambda s: acc[s], gain2)
        relay(3, 3)
        cross(3, 1)
        relay(3, 4)
        cross(3, 2)
        gather_columns(1, waits)
        clear()
        for k in range(5, 7):
            relay(3, k)
            cross(3, k - 2)
        lax.fori_loop(4, 6, functools.partial(phase_of, phase, 1), 0)
        cross(5, 5)
        cross(5, 6)
        finish(5)
        for t in range(3):
            taps(1, 2, t)
    else:
        gather_columns(0, share_edges(0, read_frame, gain1))
        clear()
        all_taps(0)
        gather_columns(1, share_edges(1, lambda s: acc[s], gain2))
        clear()
        all_taps(1)
    for s in range(slots):
        kept = jnp.where(s < count[0], read_frame(s) + acc[s], 0.0)
        out[s] = kept.astype(BF16).reshape(rows, cols, ch)
    for ok, copy in pending:
        @pl.when(ok)
        def _(copy=copy):
            copy.wait_send()
    if gathers:
        lax.fori_loop(0, 6, drain, 0)


def phase_of(phase, i, n, carry):
    return phase(i, n, carry)


def per_device(
    layout, frames, clip_lengths, group_start, group_count, kernel_one, kernel_two, gain_one, gain_two
):
    nz, ny, nr = layout
    slots, rows, cols, ch = frames.shape
    depth = kernel_one.shape[3]
    gathers = depth % 16 == 0 and (nz, ny, nr) == (4, 2, 4)
    if not gathers:
        kernel_one = lax.all_gather(kernel_one, "group", axis=3, tiled=True)
        kernel_two = lax.all_gather(kernel_two, "group", axis=3, tiled=True)
    vmem = pl.BlockSpec(memory_space=pltpu.VMEM)
    smem = pl.BlockSpec(memory_space=pltpu.SMEM)
    weight_spec = pl.BlockSpec(memory_space=pl.ANY) if gathers else vmem
    full = (6, 3, 3, ch, ch) if gathers else (16, 128)
    shards = lax.axis_size("group")
    dma = pltpu.SemaphoreType.DMA
    return pl.pallas_call(
        functools.partial(kernel, layout, gathers),
        out_shape=jax.ShapeDtypeStruct(frames.shape, BF16),
        in_specs=[vmem, weight_spec, weight_spec, vmem, vmem, smem, smem, smem],
        out_specs=vmem,
        scratch_shapes=[
            pltpu.VMEM(full, BF16),
            pltpu.VMEM((2, slots, rows, cols, ch), BF16),
            pltpu.VMEM((2, 2, rows, cols, ch), BF16),
            pltpu.VMEM((2, slots + 2, rows + 2, cols, ch), BF16),
            pltpu.VMEM((slots + 2, rows + 2, cols, 3 * ch), BF16),
            pltpu.VMEM((slots, rows * cols, ch), F32),
            dma((6, 3, shards) if gathers else (1,)),
            dma((6, shards, 6) if gathers else (1,)),
            dma((2, 5)),
            dma((2, 5)),
            dma((6,)),
        ],
        compiler_params=pltpu.CompilerParams(
            collective_id=0, has_side_effects=True, vmem_limit_bytes=56 * 1024 * 1024
        ),
    )(
        frames, kernel_one, kernel_two, gain_one, gain_two, clip_lengths, group_start, group_count
    )


def solution(mesh):
    groups, rows = mesh.shape["group"], mesh.shape["row"]
    ny = math.isqrt(groups // 2)
    return jax.shard_map(
        functools.partial(per_device, (groups // ny, ny, rows)),
        mesh=mesh,
        in_specs=(
            P("group", "row", None, None),
            P(),
            P("group"),
            P("group"),
            P(None, None, None, "group", None),
            P(None, None, None, "group", None),
            P(),
            P(),
        ),
        out_specs=P("group", "row", None, None),
        check_vma=False,
    )
```

```python
import functools
import math

import jax
import jax.numpy as jnp
from jax import lax
from jax.experimental import pallas as pl
from jax.experimental.pallas import tpu as pltpu
from jax.sharding import PartitionSpec as P

MESH = pl.DeviceIdType.MESH
BF16 = jnp.bfloat16
F32 = jnp.float32


def norm_act(data, gain):
    mean_square = jnp.mean(data * data, axis=-1, keepdims=True)
    scaled = data * lax.rsqrt(mean_square + 1e-06) * gain
    return (scaled / (1.0 + jnp.exp(-scaled))).astype(BF16)


def kernel(
    layout, gathers,
    frames, k1, k2, gain1, gain2, lengths, start, count,
    out,
    w, act, last, pad, a3, acc,
    piece_recv, piece_send, halo_recv, halo_send, own_sem,
):
    nz, ny, nr = layout
    ng = nz * ny
    slots, rows, cols, ch = frames.shape
    per = rows * cols
    g, r = lax.axis_index("group"), lax.axis_index("row")
    z, y = g // ny, g % ny
    x, c = r // 2, r % 2
    kernels = (k1, k2)
    pending = []

    always = g >= 0
    across = (always, z * ny + (1 - y), r)
    sibling = (always, g, x * 2 + (1 - c))
    other = (always, g, (1 - x) * 2 + (1 - c))

    greet = []
    if gathers:
        greet += [across, sibling, other]
        greet += [(always, (z + o) % nz * ny + y, r) for o in range(1, nz)]
    for dr in (-1, 0, 1):
        ok_r = jnp.logical_and(r + dr >= 0, r + dr < nr)
        for dg in (-1, 0, 1):
            if dr == 0 and dg == 0:
                continue
            ok = jnp.logical_and(ok_r, jnp.logical_and(g + dg >= 0, g + dg < ng))
            greet.append((ok, g + dg, r + dr))
    if gathers:
        depth = k1.shape[3]
        own = pl.ds(pl.multiple_of(g * depth, depth), depth)
        landings = [
            pltpu.make_async_copy(
                kernels[n // 3].at[:, n % 3], w.at[n, :, :, own, :], own_sem.at[n]
            )
            for n in range(6)
        ]
        for landing in landings:
            landing.start()
    barrier = pltpu.get_barrier_semaphore()
    total = 0
    for ok, tg, tr in greet:
        @pl.when(ok)
        def _(tg=tg, tr=tr):
            pl.semaphore_signal(barrier, inc=1, device_id=(tg, tr), device_id_type=MESH)
        total = total + ok.astype(jnp.int32)
    pl.semaphore_wait(barrier, total)

    def send(ok, src, dst, ssem, rsem, tg, tr):
        copy = pltpu.make_async_remote_copy(
            src_ref=src, dst_ref=dst, send_sem=ssem, recv_sem=rsem,
            device_id=(tg, tr), device_id_type=MESH,
        )

        @pl.when(ok)
        def _():
            copy.start()
        pending.append((ok, copy))

    if gathers:
        mine = 2 * c + (1 - c) * x

        def piece(n, t, s):
            return w.at[n, t, :, pl.ds(pl.multiple_of(s * depth, depth), depth), :]

        def piece_copy(n, t, s, way, to):
            there = piece(n, t, s)
            return pltpu.make_async_remote_copy(
                src_ref=there, dst_ref=there, send_sem=piece_send.at[n, s, way],
                recv_sem=piece_recv.at[n, t, s], device_id=(to[1], to[2]),
                device_id_type=MESH,
            )

        def send_piece(n, t, s, way, to):
            piece_copy(n, t, s, way, to).start()

        def sent_piece(n, t, s, way, to):
            piece_copy(n, t, s, way, to).wait_send()

        def wait_piece(n, t, s):
            piece_copy(n, t, s, 0, sibling).wait_recv()

        line = [(z + nz - o) % nz * ny + y for o in range(1, nz)]
        first = line + [z * ny + (1 - y)]
        second = [(z + nz - o) % nz * ny + (1 - y) for o in range(1, nz)]

        def own_pieces(n, act_on):
            for o in range(1, nz):
                act_on(n, mine, g, o - 1, (always, (z + o) % nz * ny + y, r))
                if o == 1:
                    act_on(n, mine, g, 3, across)

        def passed_on(n, group, act_on):
            for k, s in enumerate(group):
                if act_on is send_piece:
                    wait_piece(n, mine, s)
                if group is first and k < nz - 1:
                    act_on(n, mine, s, 0, across)

                @pl.when(c == 0)
                def _(s=s):
                    act_on(n, mine, s, 1, other)
                act_on(n, mine, s, 2, sibling)

        def relay(n, group):
            passed_on(n, group, send_piece)

        def cross(n, group):
            @pl.when(c == 1)
            def _():
                for s in group:
                    wait_piece(n, 1 - x, s)
                    send_piece(n, 1 - x, s, 3, sibling)

        def finish(n):
            for s in first + second:
                wait_piece(n, 2 * (1 - c) + c * x, s)

            @pl.when(c == 0)
            def _():
                for s in first + second:
                    wait_piece(n, 1 - x, s)

        def drain(n, carry):
            own_pieces(n, sent_piece)
            passed_on(n, first, sent_piece)
            passed_on(n, second, sent_piece)

            @pl.when(c == 1)
            def _():
                for s in first + second:
                    sent_piece(n, 1 - x, s, 3, sibling)
            return carry

        for landing in landings:
            landing.wait()
        own_pieces(0, send_piece)
        own_pieces(1, send_piece)

    def share_edges(i, read, gain):
        for s in range(slots):
            done = norm_act(read(s), gain[...][None, :]).reshape(rows, cols, ch)
            act[i, s] = done
            pad[i, 2 + s, 1 : 1 + rows] = done
        last[i] = act[i, pl.ds(jnp.clip(count[0] - 2, 0, slots - 2), 2)]

        @pl.when(r == 0)
        def _():
            pad[i, :, 0] = jnp.zeros((slots + 2, cols, ch), BF16)

        @pl.when(r == nr - 1)
        def _():
            pad[i, :, rows + 1] = jnp.zeros((slots + 2, cols, ch), BF16)

        @pl.when(g == 0)
        def _():
            pad[i, 0:2] = jnp.zeros((2, rows + 2, cols, ch), BF16)

        mine_in = pad.at[i]
        below, above, after = r < nr - 1, r > 0, g < ng - 1
        whole = pl.ds(2, slots)
        two = pl.ds(0, 2)
        plan = [
            (below, act.at[i, :, rows - 1], mine_in.at[whole, 0], g, r + 1, r > 0),
            (above, act.at[i, :, 0], mine_in.at[whole, rows + 1], g, r - 1, r < nr - 1),
            (after, last.at[i], mine_in.at[two, pl.ds(1, rows)], g + 1, r, g > 0),
            (
                jnp.logical_and(after, below), last.at[i, :, rows - 1],
                mine_in.at[two, 0], g + 1, r + 1, jnp.logical_and(g > 0, r > 0),
            ),
            (
                jnp.logical_and(after, above), last.at[i, :, 0],
                mine_in.at[two, rows + 1], g + 1, r - 1, jnp.logical_and(g > 0, r < nr - 1),
            ),
        ]
        waits = []
        for n, (ok, src, dst, tg, tr, comes) in enumerate(plan):
            send(ok, src, dst, halo_send.at[i, n], halo_recv.at[i, n], tg, tr)
            waits.append((comes, pending[-1][1]))
        return waits

    def gather_columns(i, waits):
        for comes, copy in waits:
            @pl.when(comes)
            def _(copy=copy):
                copy.wait_recv()
        size = (rows + 2) * cols
        col = lax.broadcasted_iota(jnp.int32, (size, ch), 0) % cols

        def body(f, carry):
            middle = pad[i, f].reshape(size, ch)
            wide = middle.astype(F32)
            left = jnp.where(col == 0, 0.0, pltpu.roll(wide, 1, 0)).astype(BF16)
            right = jnp.where(col == cols - 1, 0.0, pltpu.roll(wide, size - 1, 0)).astype(BF16)
            shape = (rows + 2, cols, ch)
            a3[f, :, :, 0:ch] = left.reshape(shape)
            a3[f, :, :, ch : 2 * ch] = middle.reshape(shape)
            a3[f, :, :, 2 * ch : 3 * ch] = right.reshape(shape)
            return carry

        lax.fori_loop(0, slots + 2, body, 0)

    def clear():
        acc[...] = jnp.zeros(acc.shape, F32)

    position = []
    for s in range(slots):
        frame = start[0] + s
        begin, end = jnp.int32(0), jnp.int32(0)
        for m in range(lengths.shape[0]):
            end = end + lengths[m]
            begin = jnp.where(end <= frame, jnp.maximum(begin, end), begin)
        position.append(frame - begin)

    def taps(i, p, t):
        lhs = a3[t : t + slots, pl.ds(p, rows)].reshape(slots * per, 3 * ch)
        held = w[3 * i + p, t] if gathers else kernels[i][t, p]
        part = jnp.dot(lhs, held.reshape(3 * ch, ch), preferred_element_type=F32)
        for s in range(slots):
            here = part[s * per : (s + 1) * per]
            if t < 2:
                here = here * jnp.where(position[s] >= 2 - t, 1.0, 0.0)
            acc[s] += here

    def read_frame(s):
        return frames[s].reshape(per, ch).astype(F32)

    def phase(i, n, carry):
        relay(n, first)
        cross(n - 1, second)

        @pl.when(n < 4)
        def _():
            own_pieces(n + 2, send_piece)
        finish(n - 1)
        for t in range(3):
            taps(i, n - 1 - 3 * i, t)
        relay(n, second)
        cross(n, first)
        return carry

    def all_taps(i):
        def body(p, carry):
            for t in range(3):
                taps(i, p, t)
            return carry

        lax.fori_loop(0, 3, body, 0)

    if gathers:
        waits = share_edges(0, read_frame, gain1)
        relay(0, first)
        own_pieces(2, send_piece)
        gather_columns(0, waits)
        clear()
        relay(0, second)
        cross(0, first)
        lax.fori_loop(1, 3, functools.partial(phase, 0), 0)
        relay(3, first)
        cross(2, second)
        own_pieces(5, send_piece)
        finish(2)
        for t in range(3):
            taps(0, 2, t)
        waits = share_edges(1, lambda s: acc[s], gain2)
        relay(3, second)
        cross(3, first)
        gather_columns(1, waits)
        clear()
        lax.fori_loop(4, 6, functools.partial(phase, 1), 0)
        cross(5, second)
        finish(5)
        for t in range(3):
            taps(1, 2, t)
    else:
        gather_columns(0, share_edges(0, read_frame, gain1))
        clear()
        all_taps(0)
        gather_columns(1, share_edges(1, lambda s: acc[s], gain2))
        clear()
        all_taps(1)
    for s in range(slots):
        kept = jnp.where(s < count[0], read_frame(s) + acc[s], 0.0)
        out[s] = kept.astype(BF16).reshape(rows, cols, ch)
    for ok, copy in pending:
        @pl.when(ok)
        def _(copy=copy):
            copy.wait_send()
    if gathers:
        lax.fori_loop(0, 6, drain, 0)


def per_device(
    layout, frames, clip_lengths, group_start, group_count, kernel_one, kernel_two, gain_one, gain_two
):
    nz, ny, nr = layout
    slots, rows, cols, ch = frames.shape
    depth = kernel_one.shape[3]
    gathers = depth % 16 == 0 and (nz, ny, nr) == (4, 2, 4)
    if not gathers:
        kernel_one = lax.all_gather(kernel_one, "group", axis=3, tiled=True)
        kernel_two = lax.all_gather(kernel_two, "group", axis=3, tiled=True)
    vmem = pl.BlockSpec(memory_space=pltpu.VMEM)
    smem = pl.BlockSpec(memory_space=pltpu.SMEM)
    weight_spec = pl.BlockSpec(memory_space=pl.ANY) if gathers else vmem
    full = (6, 3, 3, ch, ch) if gathers else (16, 128)
    shards = lax.axis_size("group")
    dma = pltpu.SemaphoreType.DMA
    return pl.pallas_call(
        functools.partial(kernel, layout, gathers),
        out_shape=jax.ShapeDtypeStruct(frames.shape, BF16),
        in_specs=[vmem, weight_spec, weight_spec, vmem, vmem, smem, smem, smem],
        out_specs=vmem,
        scratch_shapes=[
            pltpu.VMEM(full, BF16),
            pltpu.VMEM((2, slots, rows, cols, ch), BF16),
            pltpu.VMEM((2, 2, rows, cols, ch), BF16),
            pltpu.VMEM((2, slots + 2, rows + 2, cols, ch), BF16),
            pltpu.VMEM((slots + 2, rows + 2, cols, 3 * ch), BF16),
            pltpu.VMEM((slots, rows * cols, ch), F32),
            dma((6, 3, shards) if gathers else (1,)),
            dma((6, shards, 4) if gathers else (1,)),
            dma((2, 5)),
            dma((2, 5)),
            dma((6,)),
        ],
        compiler_params=pltpu.CompilerParams(
            collective_id=0, has_side_effects=True, vmem_limit_bytes=56 * 1024 * 1024
        ),
    )(
        frames, kernel_one, kernel_two, gain_one, gain_two, clip_lengths, group_start, group_count
    )


def solution(mesh):
    groups, rows = mesh.shape["group"], mesh.shape["row"]
    ny = math.isqrt(groups // 2)
    return jax.shard_map(
        functools.partial(per_device, (groups // ny, ny, rows)),
        mesh=mesh,
        in_specs=(
            P("group", "row", None, None),
            P(),
            P("group"),
            P("group"),
            P(None, None, None, "group", None),
            P(None, None, None, "group", None),
            P(),
            P(),
        ),
        out_specs=P("group", "row", None, None),
        check_vma=False,
    )
```

```python
import functools
import math

import jax
import jax.numpy as jnp
from jax import lax
from jax.experimental import pallas as pl
from jax.experimental.pallas import tpu as pltpu
from jax.sharding import PartitionSpec as P

MESH = pl.DeviceIdType.MESH
BF16 = jnp.bfloat16
F32 = jnp.float32


def norm_act(data, gain):
    mean_square = jnp.mean(data * data, axis=-1, keepdims=True)
    scaled = data * lax.rsqrt(mean_square + 1e-06) * gain
    return (scaled / (1.0 + jnp.exp(-scaled))).astype(BF16)


def kernel(
    layout, gathers,
    frames, k1, k2, gain1, gain2, lengths, start, count,
    out,
    w, act, last, pad, a3, acc,
    piece_recv, piece_send, halo_recv, halo_send, own_sem,
):
    nz, ny, nr = layout
    ng = nz * ny
    slots, rows, cols, ch = frames.shape
    per = rows * cols
    g, r = lax.axis_index("group"), lax.axis_index("row")
    z, y = g // ny, g % ny
    x, c = r // 2, r % 2
    kernels = (k1, k2)
    pending = []

    always = g >= 0
    across = (always, z * ny + (1 - y), r)
    sibling = (always, g, x * 2 + (1 - c))
    other = (always, g, (1 - x) * 2 + (1 - c))

    greet = []
    if gathers:
        greet += [across, sibling, other]
        greet += [(always, (z + o) % nz * ny + y, r) for o in range(1, nz)]
    for dr in (-1, 0, 1):
        ok_r = jnp.logical_and(r + dr >= 0, r + dr < nr)
        for dg in (-1, 0, 1):
            if dr == 0 and dg == 0:
                continue
            ok = jnp.logical_and(ok_r, jnp.logical_and(g + dg >= 0, g + dg < ng))
            greet.append((ok, g + dg, r + dr))
    if gathers:
        mine = 2 * c + (1 - c) * x
        landings = [
            pltpu.make_async_copy(
                kernels[n // 3].at[mine, n % 3], w.at[n, mine, :, z, y], own_sem.at[n]
            )
            for n in range(6)
        ]
        for landing in landings:
            landing.start()
    barrier = pltpu.get_barrier_semaphore()
    total = 0
    for ok, tg, tr in greet:
        @pl.when(ok)
        def _(tg=tg, tr=tr):
            pl.semaphore_signal(barrier, inc=1, device_id=(tg, tr), device_id_type=MESH)
        total = total + ok.astype(jnp.int32)
    pl.semaphore_wait(barrier, total)

    def send(ok, src, dst, ssem, rsem, tg, tr):
        copy = pltpu.make_async_remote_copy(
            src_ref=src, dst_ref=dst, send_sem=ssem, recv_sem=rsem,
            device_id=(tg, tr), device_id_type=MESH,
        )

        @pl.when(ok)
        def _():
            copy.start()
        pending.append((ok, copy))

    if gathers:
        def copy_of(n, sem, there, to):
            return pltpu.make_async_remote_copy(
                src_ref=there, dst_ref=there, send_sem=piece_send.at[n, sem],
                recv_sem=piece_recv.at[n, sem], device_id=(to[1], to[2]),
                device_id_type=MESH,
            )

        def line(n, t, row_y):
            return w.at[n, t, :, :, row_y]

        def along(n, o):
            to = (always, (z + o) % nz * ny + y, r)
            return copy_of(n, o - 1, w.at[n, mine, :, z, y], to)

        def came_along(n, o):
            there = w.at[n, mine, :, (z + nz - o) % nz, y]
            return copy_of(n, o - 1, there, sibling)

        ys = (y, 1 - y)

        def over_y(n):
            return copy_of(n, 3, line(n, mine, y), across)

        def over_x(n, k):
            return copy_of(n, 4 + k, line(n, mine, ys[k]), other)

        def to_sibling(n, k):
            return copy_of(n, 6 + k, line(n, mine, ys[k]), sibling)

        def crossed(n, k):
            return copy_of(n, 8 + k, line(n, 1 - x, ys[k]), sibling)

        def own_pieces(n):
            for o in range(1, nz):
                along(n, o).start()

        def share(n, k):
            @pl.when(c == 0)
            def _():
                over_x(n, k).start()
            to_sibling(n, k).start()

        def first(n):
            for o in range(1, nz):
                came_along(n, o).wait_recv()
            over_y(n).start()
            share(n, 0)

        def second(n):
            copy_of(n, 3, line(n, mine, 1 - y), sibling).wait_recv()
            share(n, 1)

        def cross(n, k):
            @pl.when(c == 1)
            def _():
                copy_of(n, 4 + k, line(n, 1 - x, ys[k]), sibling).wait_recv()
                crossed(n, k).start()

        def finish(n):
            for k in range(2):
                copy_of(n, 6 + k, line(n, 2 * (1 - c) + c * x, ys[k]), sibling).wait_recv()

                @pl.when(c == 0)
                def _(k=k):
                    crossed(n, k).wait_recv()

        def drain(n, carry):
            for o in range(1, nz):
                along(n, o).wait_send()
            over_y(n).wait_send()
            for k in range(2):
                to_sibling(n, k).wait_send()

                @pl.when(c == 0)
                def _(k=k):
                    over_x(n, k).wait_send()

                @pl.when(c == 1)
                def _(k=k):
                    crossed(n, k).wait_send()
            return carry

        for landing in landings:
            landing.wait()
        own_pieces(0)
        own_pieces(1)

    def share_edges(i, read, gain):
        for s in range(slots):
            done = norm_act(read(s), gain[...][None, :]).reshape(rows, cols, ch)
            act[i, s] = done
            pad[i, 2 + s, 1 : 1 + rows] = done
        last[i] = act[i, pl.ds(jnp.clip(count[0] - 2, 0, slots - 2), 2)]

        @pl.when(r == 0)
        def _():
            pad[i, :, 0] = jnp.zeros((slots + 2, cols, ch), BF16)

        @pl.when(r == nr - 1)
        def _():
            pad[i, :, rows + 1] = jnp.zeros((slots + 2, cols, ch), BF16)

        @pl.when(g == 0)
        def _():
            pad[i, 0:2] = jnp.zeros((2, rows + 2, cols, ch), BF16)

        mine_in = pad.at[i]
        below, above, after = r < nr - 1, r > 0, g < ng - 1
        whole = pl.ds(2, slots)
        two = pl.ds(0, 2)
        plan = [
            (below, act.at[i, :, rows - 1], mine_in.at[whole, 0], g, r + 1, r > 0),
            (above, act.at[i, :, 0], mine_in.at[whole, rows + 1], g, r - 1, r < nr - 1),
            (after, last.at[i], mine_in.at[two, pl.ds(1, rows)], g + 1, r, g > 0),
            (
                jnp.logical_and(after, below), last.at[i, :, rows - 1],
                mine_in.at[two, 0], g + 1, r + 1, jnp.logical_and(g > 0, r > 0),
            ),
            (
                jnp.logical_and(after, above), last.at[i, :, 0],
                mine_in.at[two, rows + 1], g + 1, r - 1, jnp.logical_and(g > 0, r < nr - 1),
            ),
        ]
        waits = []
        for n, (ok, src, dst, tg, tr, comes) in enumerate(plan):
            send(ok, src, dst, halo_send.at[i, n], halo_recv.at[i, n], tg, tr)
            waits.append((comes, pending[-1][1]))
        return waits

    def gather_columns(i, waits):
        for comes, copy in waits:
            @pl.when(comes)
            def _(copy=copy):
                copy.wait_recv()
        size = (rows + 2) * cols
        col = lax.broadcasted_iota(jnp.int32, (size, ch), 0) % cols

        def body(f, carry):
            middle = pad[i, f].reshape(size, ch)
            wide = middle.astype(F32)
            left = jnp.where(col == 0, 0.0, pltpu.roll(wide, 1, 0)).astype(BF16)
            right = jnp.where(col == cols - 1, 0.0, pltpu.roll(wide, size - 1, 0)).astype(BF16)
            shape = (rows + 2, cols, ch)
            a3[f, :, :, 0:ch] = left.reshape(shape)
            a3[f, :, :, ch : 2 * ch] = middle.reshape(shape)
            a3[f, :, :, 2 * ch : 3 * ch] = right.reshape(shape)
            return carry

        lax.fori_loop(0, slots + 2, body, 0)

    def clear():
        acc[...] = jnp.zeros(acc.shape, F32)

    position = []
    for s in range(slots):
        frame = start[0] + s
        begin, end = jnp.int32(0), jnp.int32(0)
        for m in range(lengths.shape[0]):
            end = end + lengths[m]
            begin = jnp.where(end <= frame, jnp.maximum(begin, end), begin)
        position.append(frame - begin)

    def taps(i, p):
        def body(t, carry):
            lhs = a3[pl.ds(t, slots), p : p + rows].reshape(slots * per, 3 * ch)
            held = w[3 * i + p, t] if gathers else kernels[i][t, p]
            part = jnp.dot(lhs, held.reshape(3 * ch, ch), preferred_element_type=F32)
            for s in range(slots):
                kept = jnp.where(position[s] >= 2 - t, 1.0, 0.0)
                acc[s] += part[s * per : (s + 1) * per] * kept
            return carry

        lax.fori_loop(0, 3, body, 0)

    def read_frame(s):
        return frames[s].reshape(per, ch).astype(F32)

    for n in range(8):
        if gathers:
            if n == 0:
                waits = share_edges(0, read_frame, gain1)
            if n < 6:
                first(n)
            if n + 2 < 6:
                own_pieces(n + 2)
            if 0 <= n - 1 < 6:
                second(n - 1)
                cross(n - 1, 0)
            if n >= 2:
                cross(n - 2, 1)
                finish(n - 2)
        elif n == 0:
            waits = share_edges(0, read_frame, gain1)
        if n == 0:
            gather_columns(0, waits)
            clear()
        if n == 5:
            gather_columns(1, waits)
            clear()
        if n >= 2:
            taps((n - 2) // 3, (n - 2) % 3)
        if n == 4:
            waits = share_edges(1, lambda s: acc[s], gain2)
    for s in range(slots):
        kept = jnp.where(s < count[0], read_frame(s) + acc[s], 0.0)
        out[s] = kept.astype(BF16).reshape(rows, cols, ch)
    for ok, copy in pending:
        @pl.when(ok)
        def _(copy=copy):
            copy.wait_send()
    if gathers:
        lax.fori_loop(0, 6, drain, 0)


def per_device(
    layout, frames, clip_lengths, group_start, group_count, kernel_one, kernel_two, gain_one, gain_two
):
    nz, ny, nr = layout
    slots, rows, cols, ch = frames.shape
    depth = kernel_one.shape[3]
    gathers = depth % 16 == 0 and (nz, ny, nr) == (4, 2, 4)
    if not gathers:
        kernel_one = lax.all_gather(kernel_one, "group", axis=3, tiled=True)
        kernel_two = lax.all_gather(kernel_two, "group", axis=3, tiled=True)
    vmem = pl.BlockSpec(memory_space=pltpu.VMEM)
    smem = pl.BlockSpec(memory_space=pltpu.SMEM)
    weight_spec = pl.BlockSpec(memory_space=pl.ANY) if gathers else vmem
    full = (6, 3, 3, nz, ny, depth, ch) if gathers else (16, 128)
    dma = pltpu.SemaphoreType.DMA
    return pl.pallas_call(
        functools.partial(kernel, layout, gathers),
        out_shape=jax.ShapeDtypeStruct(frames.shape, BF16),
        in_specs=[vmem, weight_spec, weight_spec, vmem, vmem, smem, smem, smem],
        out_specs=vmem,
        scratch_shapes=[
            pltpu.VMEM(full, BF16),
            pltpu.VMEM((2, slots, rows, cols, ch), BF16),
            pltpu.VMEM((2, 2, rows, cols, ch), BF16),
            pltpu.VMEM((2, slots + 2, rows + 2, cols, ch), BF16),
            pltpu.VMEM((slots + 2, rows + 2, cols, 3 * ch), BF16),
            pltpu.VMEM((slots, rows * cols, ch), F32),
            dma((6, 10) if gathers else (1,)),
            dma((6, 10) if gathers else (1,)),
            dma((2, 5)),
            dma((2, 5)),
            dma((6,)),
        ],
        compiler_params=pltpu.CompilerParams(
            collective_id=0, has_side_effects=True, vmem_limit_bytes=56 * 1024 * 1024
        ),
    )(
        frames, kernel_one, kernel_two, gain_one, gain_two, clip_lengths, group_start, group_count
    )


def solution(mesh):
    groups, rows = mesh.shape["group"], mesh.shape["row"]
    ny = math.isqrt(groups // 2)
    return jax.shard_map(
        functools.partial(per_device, (groups // ny, ny, rows)),
        mesh=mesh,
        in_specs=(
            P("group", "row", None, None),
            P(),
            P("group"),
            P("group"),
            P(None, None, None, "group", None),
            P(None, None, None, "group", None),
            P(),
            P(),
        ),
        out_specs=P("group", "row", None, None),
        check_vma=False,
    )
```

```python
import functools
import math

import jax
import jax.numpy as jnp
from jax import lax
from jax.experimental import pallas as pl
from jax.experimental.pallas import tpu as pltpu
from jax.sharding import PartitionSpec as P

MESH = pl.DeviceIdType.MESH
BF16 = jnp.bfloat16
F32 = jnp.float32


def norm_act(data, gain):
    mean_square = jnp.mean(data * data, axis=-1, keepdims=True)
    scaled = data * lax.rsqrt(mean_square + 1e-06) * gain
    return (scaled / (1.0 + jnp.exp(-scaled))).astype(BF16)


def kernel(
    layout, gathers,
    frames, k1, k2, gain1, gain2, lengths, start, count,
    out,
    w, act, last, pad, a3, acc,
    piece_recv, piece_send, halo_recv, halo_send, own_sem,
):
    nz, ny, nr = layout
    ng = nz * ny
    slots, rows, cols, ch = frames.shape
    per = rows * cols
    g, r = lax.axis_index("group"), lax.axis_index("row")
    z, y = g // ny, g % ny
    x, c = r // 2, r % 2
    kernels = (k1, k2)
    pending = []

    always = g >= 0
    across = (always, z * ny + (1 - y), r)
    sibling = (always, g, x * 2 + (1 - c))
    other = (always, g, (1 - x) * 2 + (1 - c))

    greet = []
    if gathers:
        greet += [across, sibling, other, (always, g, (1 - x) * 2 + c)]
        greet += [(always, (z + o) % nz * ny + y, r) for o in range(1, nz)]
    for dr in (-1, 0, 1):
        ok_r = jnp.logical_and(r + dr >= 0, r + dr < nr)
        for dg in (-1, 0, 1):
            if dr == 0 and dg == 0:
                continue
            ok = jnp.logical_and(ok_r, jnp.logical_and(g + dg >= 0, g + dg < ng))
            greet.append((ok, g + dg, r + dr))
    if gathers:
        depth = k1.shape[3]
        own = pl.ds(pl.multiple_of(g * depth, depth), depth)
        landings = [
            pltpu.make_async_copy(
                kernels[n // 3].at[:, n % 3], w.at[n, :, :, own, :], own_sem.at[n]
            )
            for n in range(6)
        ]
        for landing in landings:
            landing.start()
    barrier = pltpu.get_barrier_semaphore()
    total = 0
    for ok, tg, tr in greet:
        @pl.when(ok)
        def _(tg=tg, tr=tr):
            pl.semaphore_signal(barrier, inc=1, device_id=(tg, tr), device_id_type=MESH)
        total = total + ok.astype(jnp.int32)
    pl.semaphore_wait(barrier, total)

    def send(ok, src, dst, ssem, rsem, tg, tr):
        copy = pltpu.make_async_remote_copy(
            src_ref=src, dst_ref=dst, send_sem=ssem, recv_sem=rsem,
            device_id=(tg, tr), device_id_type=MESH,
        )

        @pl.when(ok)
        def _():
            copy.start()
        pending.append((ok, copy))

    if gathers:
        mine = 2 * c + (1 - c) * x

        def piece(n, t, s):
            return w.at[n, t, :, pl.ds(pl.multiple_of(s * depth, depth), depth), :]

        def piece_copy(n, t, s, way, to):
            there = piece(n, t, s)
            return pltpu.make_async_remote_copy(
                src_ref=there, dst_ref=there, send_sem=piece_send.at[n, s, way],
                recv_sem=piece_recv.at[n, t, s], device_id=(to[1], to[2]),
                device_id_type=MESH,
            )

        def send_piece(n, t, s, way, to):
            piece_copy(n, t, s, way, to).start()

        def sent_piece(n, t, s, way, to):
            piece_copy(n, t, s, way, to).wait_send()

        def wait_piece(n, t, s):
            piece_copy(n, t, s, 0, sibling).wait_recv()

        gaps = [jnp.where(z < 2, nz - o, o) for o in range(1, nz)]
        line = [(z + nz - gap) % nz * ny + y for gap in gaps]
        inner = jnp.logical_and(z > 0, z < nz - 1)
        far_end = (always, (nz - 1) * (z - 1) * ny + y, r)
        level = (always, g, (1 - x) * 2 + c)
        first = line + [z * ny + (1 - y)]
        second = [(z + nz - gap) % nz * ny + (1 - y) for gap in gaps]

        def own_pieces(n, act_on):
            for o in range(1, nz):
                zz = (z + o) % nz

                @pl.when(jnp.abs(zz - z) < nz - 1)
                def _(o=o, zz=zz):
                    act_on(n, mine, g, o - 1, (always, zz * ny + y, r))
                if o == 1:
                    act_on(n, mine, g, 3, across)

        def in_turn(n):
            return (n + x) % 2 == 0

        def passed_on(n, group, act_on):
            for k, s in enumerate(group):
                if act_on is send_piece:
                    wait_piece(n, mine, s)
                if group is first and k == 1:
                    @pl.when(inner)
                    def _(s=s):
                        act_on(n, mine, s, 4, far_end)

                    @pl.when(jnp.logical_or(c == 0, in_turn(n)))
                    def _(s=s):
                        act_on(n, mine, s, 0, across)
                elif group is first and k < nz - 1:
                    act_on(n, mine, s, 0, across)
                if group is second and k == 1:
                    @pl.when(jnp.logical_and(c == 1, in_turn(n)))
                    def _(s=s):
                        act_on(n, mine, s, 4, level)

                @pl.when(c == 0)
                def _(s=s):
                    act_on(n, mine, s, 1, other)
                act_on(n, mine, s, 2, sibling)

        def relay(n, group):
            passed_on(n, group, send_piece)

        def cross(n, group):
            @pl.when(c == 1)
            def _():
                for s in group:
                    wait_piece(n, 1 - x, s)
                    send_piece(n, 1 - x, s, 3, sibling)

        def finish(n):
            for s in first + second:
                wait_piece(n, 2 * (1 - c) + c * x, s)

            @pl.when(c == 0)
            def _():
                for s in first + second:
                    wait_piece(n, 1 - x, s)

        def drain(n, carry):
            own_pieces(n, sent_piece)
            passed_on(n, first, sent_piece)
            passed_on(n, second, sent_piece)

            @pl.when(c == 1)
            def _():
                for s in first + second:
                    sent_piece(n, 1 - x, s, 3, sibling)
            return carry

        for landing in landings:
            landing.wait()
        own_pieces(0, send_piece)
        own_pieces(1, send_piece)

    def share_edges(i, read, gain):
        for s in range(slots):
            done = norm_act(read(s), gain[...][None, :]).reshape(rows, cols, ch)
            act[i, s] = done
            pad[i, 2 + s, 1 : 1 + rows] = done
        last[i] = act[i, pl.ds(jnp.clip(count[0] - 2, 0, slots - 2), 2)]

        @pl.when(r == 0)
        def _():
            pad[i, :, 0] = jnp.zeros((slots + 2, cols, ch), BF16)

        @pl.when(r == nr - 1)
        def _():
            pad[i, :, rows + 1] = jnp.zeros((slots + 2, cols, ch), BF16)

        @pl.when(g == 0)
        def _():
            pad[i, 0:2] = jnp.zeros((2, rows + 2, cols, ch), BF16)

        mine_in = pad.at[i]
        below, above, after = r < nr - 1, r > 0, g < ng - 1
        whole = pl.ds(2, slots)
        two = pl.ds(0, 2)
        plan = [
            (below, act.at[i, :, rows - 1], mine_in.at[whole, 0], g, r + 1, r > 0),
            (above, act.at[i, :, 0], mine_in.at[whole, rows + 1], g, r - 1, r < nr - 1),
            (after, last.at[i], mine_in.at[two, pl.ds(1, rows)], g + 1, r, g > 0),
            (
                jnp.logical_and(after, below), last.at[i, :, rows - 1],
                mine_in.at[two, 0], g + 1, r + 1, jnp.logical_and(g > 0, r > 0),
            ),
            (
                jnp.logical_and(after, above), last.at[i, :, 0],
                mine_in.at[two, rows + 1], g + 1, r - 1, jnp.logical_and(g > 0, r < nr - 1),
            ),
        ]
        waits = []
        for n, (ok, src, dst, tg, tr, comes) in enumerate(plan):
            send(ok, src, dst, halo_send.at[i, n], halo_recv.at[i, n], tg, tr)
            waits.append((comes, pending[-1][1]))
        return waits

    def gather_columns(i, waits):
        for comes, copy in waits:
            @pl.when(comes)
            def _(copy=copy):
                copy.wait_recv()
        size = (rows + 2) * cols
        col = lax.broadcasted_iota(jnp.int32, (size, ch), 0) % cols

        def body(f, carry):
            middle = pad[i, f].reshape(size, ch)
            wide = middle.astype(F32)
            left = jnp.where(col == 0, 0.0, pltpu.roll(wide, 1, 0)).astype(BF16)
            right = jnp.where(col == cols - 1, 0.0, pltpu.roll(wide, size - 1, 0)).astype(BF16)
            shape = (rows + 2, cols, ch)
            a3[f, :, :, 0:ch] = left.reshape(shape)
            a3[f, :, :, ch : 2 * ch] = middle.reshape(shape)
            a3[f, :, :, 2 * ch : 3 * ch] = right.reshape(shape)
            return carry

        lax.fori_loop(0, slots + 2, body, 0)

    def clear():
        acc[...] = jnp.zeros(acc.shape, F32)

    position = []
    for s in range(slots):
        frame = start[0] + s
        begin, end = jnp.int32(0), jnp.int32(0)
        for m in range(lengths.shape[0]):
            end = end + lengths[m]
            begin = jnp.where(end <= frame, jnp.maximum(begin, end), begin)
        position.append(frame - begin)

    def taps(i, p, t):
        lhs = a3[t : t + slots, pl.ds(p, rows)].reshape(slots * per, 3 * ch)
        held = w[3 * i + p, t] if gathers else kernels[i][t, p]
        part = jnp.dot(lhs, held.reshape(3 * ch, ch), preferred_element_type=F32)
        for s in range(slots):
            here = part[s * per : (s + 1) * per]
            if t < 2:
                here = here * jnp.where(position[s] >= 2 - t, 1.0, 0.0)
            acc[s] += here

    def read_frame(s):
        return frames[s].reshape(per, ch).astype(F32)

    def phase(i, n, carry):
        relay(n, first)
        cross(n - 1, second)

        @pl.when(n < 4)
        def _():
            own_pieces(n + 2, send_piece)
        finish(n - 1)
        for t in range(3):
            taps(i, n - 1 - 3 * i, t)
        relay(n, second)
        cross(n, first)
        return carry

    def all_taps(i):
        def body(p, carry):
            for t in range(3):
                taps(i, p, t)
            return carry

        lax.fori_loop(0, 3, body, 0)

    if gathers:
        waits = share_edges(0, read_frame, gain1)
        relay(0, first)
        own_pieces(2, send_piece)
        gather_columns(0, waits)
        clear()
        relay(0, second)
        cross(0, first)
        lax.fori_loop(1, 3, functools.partial(phase, 0), 0)
        relay(3, first)
        cross(2, second)
        own_pieces(5, send_piece)
        finish(2)
        for t in range(3):
            taps(0, 2, t)
        waits = share_edges(1, lambda s: acc[s], gain2)
        relay(3, second)
        cross(3, first)
        gather_columns(1, waits)
        clear()
        lax.fori_loop(4, 6, functools.partial(phase, 1), 0)
        cross(5, second)
        finish(5)
        for t in range(3):
            taps(1, 2, t)
    else:
        gather_columns(0, share_edges(0, read_frame, gain1))
        clear()
        all_taps(0)
        gather_columns(1, share_edges(1, lambda s: acc[s], gain2))
        clear()
        all_taps(1)
    for s in range(slots):
        kept = jnp.where(s < count[0], read_frame(s) + acc[s], 0.0)
        out[s] = kept.astype(BF16).reshape(rows, cols, ch)
    for ok, copy in pending:
        @pl.when(ok)
        def _(copy=copy):
            copy.wait_send()
    if gathers:
        lax.fori_loop(0, 6, drain, 0)


def per_device(
    layout, frames, clip_lengths, group_start, group_count, kernel_one, kernel_two, gain_one, gain_two
):
    nz, ny, nr = layout
    slots, rows, cols, ch = frames.shape
    depth = kernel_one.shape[3]
    gathers = depth % 16 == 0 and (nz, ny, nr) == (4, 2, 4)
    if not gathers:
        kernel_one = lax.all_gather(kernel_one, "group", axis=3, tiled=True)
        kernel_two = lax.all_gather(kernel_two, "group", axis=3, tiled=True)
    vmem = pl.BlockSpec(memory_space=pltpu.VMEM)
    smem = pl.BlockSpec(memory_space=pltpu.SMEM)
    weight_spec = pl.BlockSpec(memory_space=pl.ANY) if gathers else vmem
    full = (6, 3, 3, ch, ch) if gathers else (16, 128)
    shards = lax.axis_size("group")
    dma = pltpu.SemaphoreType.DMA
    return pl.pallas_call(
        functools.partial(kernel, layout, gathers),
        out_shape=jax.ShapeDtypeStruct(frames.shape, BF16),
        in_specs=[vmem, weight_spec, weight_spec, vmem, vmem, smem, smem, smem],
        out_specs=vmem,
        scratch_shapes=[
            pltpu.VMEM(full, BF16),
            pltpu.VMEM((2, slots, rows, cols, ch), BF16),
            pltpu.VMEM((2, 2, rows, cols, ch), BF16),
            pltpu.VMEM((2, slots + 2, rows + 2, cols, ch), BF16),
            pltpu.VMEM((slots + 2, rows + 2, cols, 3 * ch), BF16),
            pltpu.VMEM((slots, rows * cols, ch), F32),
            dma((6, 3, shards) if gathers else (1,)),
            dma((6, shards, 5) if gathers else (1,)),
            dma((2, 5)),
            dma((2, 5)),
            dma((6,)),
        ],
        compiler_params=pltpu.CompilerParams(
            collective_id=0, has_side_effects=True, vmem_limit_bytes=56 * 1024 * 1024
        ),
    )(
        frames, kernel_one, kernel_two, gain_one, gain_two, clip_lengths, group_start, group_count
    )


def solution(mesh):
    groups, rows = mesh.shape["group"], mesh.shape["row"]
    ny = math.isqrt(groups // 2)
    return jax.shard_map(
        functools.partial(per_device, (groups // ny, ny, rows)),
        mesh=mesh,
        in_specs=(
            P("group", "row", None, None),
            P(),
            P("group"),
            P("group"),
            P(None, None, None, "group", None),
            P(None, None, None, "group", None),
            P(),
            P(),
        ),
        out_specs=P("group", "row", None, None),
        check_vma=False,
    )
```

```python
import functools
import math

import jax
import jax.numpy as jnp
from jax import lax
from jax.experimental import pallas as pl
from jax.experimental.pallas import tpu as pltpu
from jax.sharding import PartitionSpec as P

MESH = pl.DeviceIdType.MESH
BF16 = jnp.bfloat16
F32 = jnp.float32


def norm_act(data, gain):
    mean_square = jnp.mean(data * data, axis=-1, keepdims=True)
    scaled = data * lax.rsqrt(mean_square + 1e-06) * gain
    return (scaled / (1.0 + jnp.exp(-scaled))).astype(BF16)


def kernel(
    layout, gathers,
    frames, k1, k2, gain1, gain2, lengths, start, count,
    out,
    w, act, last, pad, a3, acc,
    piece_recv, piece_send, halo_recv, halo_send, own_sem,
):
    nz, ny, nr = layout
    ng = nz * ny
    slots, rows, cols, ch = frames.shape
    per = rows * cols
    g, r = lax.axis_index("group"), lax.axis_index("row")
    z, y = g // ny, g % ny
    x, c = r // 2, r % 2
    kernels = (k1, k2)
    pending = []

    always = g >= 0
    across = (always, z * ny + (1 - y), r)
    sibling = (always, g, x * 2 + (1 - c))
    other = (always, g, (1 - x) * 2 + (1 - c))

    greet = []
    if gathers:
        greet += [across, sibling, other, (always, g, (1 - x) * 2 + c)]
        greet += [(always, (z + o) % nz * ny + y, r) for o in range(1, nz)]
    for dr in (-1, 0, 1):
        ok_r = jnp.logical_and(r + dr >= 0, r + dr < nr)
        for dg in (-1, 0, 1):
            if dr == 0 and dg == 0:
                continue
            ok = jnp.logical_and(ok_r, jnp.logical_and(g + dg >= 0, g + dg < ng))
            greet.append((ok, g + dg, r + dr))
    if gathers:
        depth = k1.shape[3]
        own = pl.ds(pl.multiple_of(g * depth, depth), depth)
        landings = [
            pltpu.make_async_copy(
                kernels[n // 3].at[:, n % 3], w.at[n, :, :, own, :], own_sem.at[n]
            )
            for n in range(6)
        ]
        for landing in landings:
            landing.start()
    barrier = pltpu.get_barrier_semaphore()
    total = 0
    for ok, tg, tr in greet:
        @pl.when(ok)
        def _(tg=tg, tr=tr):
            pl.semaphore_signal(barrier, inc=1, device_id=(tg, tr), device_id_type=MESH)
        total = total + ok.astype(jnp.int32)
    pl.semaphore_wait(barrier, total)

    def send(ok, src, dst, ssem, rsem, tg, tr):
        copy = pltpu.make_async_remote_copy(
            src_ref=src, dst_ref=dst, send_sem=ssem, recv_sem=rsem,
            device_id=(tg, tr), device_id_type=MESH,
        )

        @pl.when(ok)
        def _():
            copy.start()
        pending.append((ok, copy))

    if gathers:
        mine = 2 * c + (1 - c) * x

        def piece(n, t, s):
            return w.at[n, t, :, pl.ds(pl.multiple_of(s * depth, depth), depth), :]

        def piece_copy(n, t, s, way, to):
            there = piece(n, t, s)
            return pltpu.make_async_remote_copy(
                src_ref=there, dst_ref=there, send_sem=piece_send.at[n, s, way],
                recv_sem=piece_recv.at[n, t, s], device_id=(to[1], to[2]),
                device_id_type=MESH,
            )

        def send_piece(n, t, s, way, to):
            piece_copy(n, t, s, way, to).start()

        def sent_piece(n, t, s, way, to):
            piece_copy(n, t, s, way, to).wait_send()

        def wait_piece(n, t, s):
            piece_copy(n, t, s, 0, sibling).wait_recv()

        gaps = [jnp.where(z < 2, nz - o, o) for o in range(1, nz)]
        line = [(z + nz - gap) % nz * ny + y for gap in gaps]
        inner = jnp.logical_and(z > 0, z < nz - 1)
        far_end = (always, (nz - 1) * (z - 1) * ny + y, r)
        level = (always, g, (1 - x) * 2 + c)
        first = line + [z * ny + (1 - y)]
        second = [(z + nz - gap) % nz * ny + (1 - y) for gap in gaps]

        def own_pieces(n, act_on):
            for o in range(1, nz):
                zz = (z + o) % nz

                @pl.when(jnp.abs(zz - z) < nz - 1)
                def _(o=o, zz=zz):
                    act_on(n, mine, g, o - 1, (always, zz * ny + y, r))
                if o == 1:
                    act_on(n, mine, g, 3, across)

        def in_turn(n):
            return (n + x) % 2 == 0

        def passed_on(n, group, act_on):
            for k, s in enumerate(group):
                if act_on is send_piece:
                    wait_piece(n, mine, s)
                if group is first and k == 1:
                    @pl.when(inner)
                    def _(s=s):
                        act_on(n, mine, s, 4, far_end)

                    @pl.when(jnp.logical_or(c == 0, in_turn(n)))
                    def _(s=s):
                        act_on(n, mine, s, 0, across)
                elif group is first and k < nz - 1:
                    act_on(n, mine, s, 0, across)
                if group is second and k == 1:
                    @pl.when(jnp.logical_and(c == 1, in_turn(n)))
                    def _(s=s):
                        act_on(n, mine, s, 4, level)

                @pl.when(c == 0)
                def _(s=s):
                    act_on(n, mine, s, 1, other)
                act_on(n, mine, s, 2, sibling)

        def relay(n, group):
            passed_on(n, group, send_piece)

        def cross(n, group):
            @pl.when(c == 1)
            def _():
                for s in group:
                    wait_piece(n, 1 - x, s)
                    send_piece(n, 1 - x, s, 3, sibling)

        def finish(n):
            for s in first + second:
                wait_piece(n, 2 * (1 - c) + c * x, s)

            @pl.when(c == 0)
            def _():
                for s in first + second:
                    wait_piece(n, 1 - x, s)

        def drain(n, carry):
            own_pieces(n, sent_piece)
            passed_on(n, first, sent_piece)
            passed_on(n, second, sent_piece)

            @pl.when(c == 1)
            def _():
                for s in first + second:
                    sent_piece(n, 1 - x, s, 3, sibling)
            return carry

        for landing in landings:
            landing.wait()
        own_pieces(0, send_piece)
        own_pieces(1, send_piece)

    def share_edges(i, read, gain):
        for s in range(slots):
            done = norm_act(read(s), gain[...][None, :]).reshape(rows, cols, ch)
            act[i, s] = done
            pad[i, 2 + s, 1 : 1 + rows] = done
        last[i] = act[i, pl.ds(jnp.clip(count[0] - 2, 0, slots - 2), 2)]

        @pl.when(r == 0)
        def _():
            pad[i, :, 0] = jnp.zeros((slots + 2, cols, ch), BF16)

        @pl.when(r == nr - 1)
        def _():
            pad[i, :, rows + 1] = jnp.zeros((slots + 2, cols, ch), BF16)

        @pl.when(g == 0)
        def _():
            pad[i, 0:2] = jnp.zeros((2, rows + 2, cols, ch), BF16)

        mine_in = pad.at[i]
        below, above, after = r < nr - 1, r > 0, g < ng - 1
        whole = pl.ds(2, slots)
        two = pl.ds(0, 2)
        plan = [
            (below, act.at[i, :, rows - 1], mine_in.at[whole, 0], g, r + 1, r > 0),
            (above, act.at[i, :, 0], mine_in.at[whole, rows + 1], g, r - 1, r < nr - 1),
            (after, last.at[i], mine_in.at[two, pl.ds(1, rows)], g + 1, r, g > 0),
            (
                jnp.logical_and(after, below), last.at[i, :, rows - 1],
                mine_in.at[two, 0], g + 1, r + 1, jnp.logical_and(g > 0, r > 0),
            ),
            (
                jnp.logical_and(after, above), last.at[i, :, 0],
                mine_in.at[two, rows + 1], g + 1, r - 1, jnp.logical_and(g > 0, r < nr - 1),
            ),
        ]
        waits = []
        for n, (ok, src, dst, tg, tr, comes) in enumerate(plan):
            send(ok, src, dst, halo_send.at[i, n], halo_recv.at[i, n], tg, tr)
            waits.append((comes, pending[-1][1]))
        return waits

    def gather_columns(i, waits):
        for comes, copy in waits:
            @pl.when(comes)
            def _(copy=copy):
                copy.wait_recv()
        size = (rows + 2) * cols
        col = lax.broadcasted_iota(jnp.int32, (size, ch), 0) % cols

        def body(f, carry):
            middle = pad[i, f].reshape(size, ch)
            wide = middle.astype(F32)
            left = jnp.where(col == 0, 0.0, pltpu.roll(wide, 1, 0)).astype(BF16)
            right = jnp.where(col == cols - 1, 0.0, pltpu.roll(wide, size - 1, 0)).astype(BF16)
            shape = (rows + 2, cols, ch)
            a3[f, :, :, 0:ch] = left.reshape(shape)
            a3[f, :, :, ch : 2 * ch] = middle.reshape(shape)
            a3[f, :, :, 2 * ch : 3 * ch] = right.reshape(shape)
            return carry

        lax.fori_loop(0, slots + 2, body, 0)

    def clear():
        acc[...] = jnp.zeros(acc.shape, F32)

    position = []
    for s in range(slots):
        frame = start[0] + s
        begin, end = jnp.int32(0), jnp.int32(0)
        for m in range(lengths.shape[0]):
            end = end + lengths[m]
            begin = jnp.where(end <= frame, jnp.maximum(begin, end), begin)
        position.append(frame - begin)

    def taps(i, p):
        def body(t, carry):
            lhs = a3[pl.ds(t, slots), pl.ds(p, rows)].reshape(slots * per, 3 * ch)
            held = w[3 * i + p, t] if gathers else kernels[i][t, p]
            part = jnp.dot(lhs, held.reshape(3 * ch, ch), preferred_element_type=F32)
            for s in range(slots):
                kept = jnp.where(position[s] >= 2 - t, 1.0, 0.0)
                acc[s] += part[s * per : (s + 1) * per] * kept
            return carry

        lax.fori_loop(0, 3, body, 0)

    def read_frame(s):
        return frames[s].reshape(per, ch).astype(F32)

    def tick(n, more):
        relay(n, first)
        if more:
            own_pieces(n + 2, send_piece)
        relay(n - 1, second)
        cross(n - 1, first)
        cross(n - 2, second)
        finish(n - 2)

    def early(n, carry):
        tick(n, True)
        taps(0, n - 2)
        return carry

    def all_taps(i):
        def body(p, carry):
            taps(i, p)
            return carry

        lax.fori_loop(0, 3, body, 0)

    def edges_again():
        return share_edges(1, lambda s: acc[s], gain2)

    waits = share_edges(0, read_frame, gain1)
    if gathers:
        relay(0, first)
        own_pieces(2, send_piece)
        gather_columns(0, waits)
        clear()
        relay(1, first)
        own_pieces(3, send_piece)
        relay(0, second)
        cross(0, first)
        lax.fori_loop(2, 4, early, 0)
        tick(4, False)
        taps(0, 2)
        waits = edges_again()
        tick(5, False)
        gather_columns(1, waits)
        clear()
        taps(1, 0)
        relay(5, second)
        cross(5, first)
        cross(4, second)
        finish(4)
        taps(1, 1)
        cross(5, second)
        finish(5)
        taps(1, 2)
    else:
        gather_columns(0, waits)
        clear()
        all_taps(0)
        gather_columns(1, edges_again())
        clear()
        all_taps(1)
    for s in range(slots):
        kept = jnp.where(s < count[0], read_frame(s) + acc[s], 0.0)
        out[s] = kept.astype(BF16).reshape(rows, cols, ch)
    for ok, copy in pending:
        @pl.when(ok)
        def _(copy=copy):
            copy.wait_send()
    if gathers:
        lax.fori_loop(0, 6, drain, 0)


def per_device(
    layout, frames, clip_lengths, group_start, group_count, kernel_one, kernel_two, gain_one, gain_two
):
    nz, ny, nr = layout
    slots, rows, cols, ch = frames.shape
    depth = kernel_one.shape[3]
    gathers = depth % 16 == 0 and (nz, ny, nr) == (4, 2, 4)
    if not gathers:
        kernel_one = lax.all_gather(kernel_one, "group", axis=3, tiled=True)
        kernel_two = lax.all_gather(kernel_two, "group", axis=3, tiled=True)
    vmem = pl.BlockSpec(memory_space=pltpu.VMEM)
    smem = pl.BlockSpec(memory_space=pltpu.SMEM)
    weight_spec = pl.BlockSpec(memory_space=pl.ANY) if gathers else vmem
    full = (6, 3, 3, ch, ch) if gathers else (16, 128)
    shards = lax.axis_size("group")
    dma = pltpu.SemaphoreType.DMA
    return pl.pallas_call(
        functools.partial(kernel, layout, gathers),
        out_shape=jax.ShapeDtypeStruct(frames.shape, BF16),
        in_specs=[vmem, weight_spec, weight_spec, vmem, vmem, smem, smem, smem],
        out_specs=vmem,
        scratch_shapes=[
            pltpu.VMEM(full, BF16),
            pltpu.VMEM((2, slots, rows, cols, ch), BF16),
            pltpu.VMEM((2, 2, rows, cols, ch), BF16),
            pltpu.VMEM((2, slots + 2, rows + 2, cols, ch), BF16),
            pltpu.VMEM((slots + 2, rows + 2, cols, 3 * ch), BF16),
            pltpu.VMEM((slots, rows * cols, ch), F32),
            dma((6, 3, shards) if gathers else (1,)),
            dma((6, shards, 5) if gathers else (1,)),
            dma((2, 5)),
            dma((2, 5)),
            dma((6,)),
        ],
        compiler_params=pltpu.CompilerParams(
            collective_id=0, has_side_effects=True, vmem_limit_bytes=56 * 1024 * 1024
        ),
    )(
        frames, kernel_one, kernel_two, gain_one, gain_two, clip_lengths, group_start, group_count
    )


def solution(mesh):
    groups, rows = mesh.shape["group"], mesh.shape["row"]
    ny = math.isqrt(groups // 2)
    return jax.shard_map(
        functools.partial(per_device, (groups // ny, ny, rows)),
        mesh=mesh,
        in_specs=(
            P("group", "row", None, None),
            P(),
            P("group"),
            P("group"),
            P(None, None, None, "group", None),
            P(None, None, None, "group", None),
            P(),
            P(),
        ),
        out_specs=P("group", "row", None, None),
        check_vma=False,
    )
```

```python
import functools
import math

import jax
import jax.numpy as jnp
from jax import lax
from jax.experimental import pallas as pl
from jax.experimental.pallas import tpu as pltpu
from jax.sharding import PartitionSpec as P

MESH = pl.DeviceIdType.MESH
BF16 = jnp.bfloat16
F32 = jnp.float32


def norm_act(data, gain):
    mean_square = jnp.mean(data * data, axis=-1, keepdims=True)
    scaled = data * lax.rsqrt(mean_square + 1e-06) * gain
    return (scaled / (1.0 + jnp.exp(-scaled))).astype(BF16)


def kernel(
    layout, gathers,
    frames, k1, k2, gain1, gain2, lengths, start, count,
    out,
    w, act, last, pad, a3, acc,
    piece_recv, piece_send, halo_recv, halo_send, own_sem,
):
    nz, ny, nr = layout
    ng = nz * ny
    slots, rows, cols, ch = frames.shape
    per = rows * cols
    g, r = lax.axis_index("group"), lax.axis_index("row")
    z, y = g // ny, g % ny
    x, c = r // 2, r % 2
    kernels = (k1, k2)
    pending = []

    always = g >= 0
    across = (always, z * ny + (1 - y), r)
    sibling = (always, g, x * 2 + (1 - c))
    other = (always, g, (1 - x) * 2 + (1 - c))

    greet = []
    if gathers:
        greet += [across, sibling, other]
        greet += [(always, (z + o) % nz * ny + y, r) for o in range(1, nz)]
    for dr in (-1, 0, 1):
        ok_r = jnp.logical_and(r + dr >= 0, r + dr < nr)
        for dg in (-1, 0, 1):
            if dr == 0 and dg == 0:
                continue
            ok = jnp.logical_and(ok_r, jnp.logical_and(g + dg >= 0, g + dg < ng))
            greet.append((ok, g + dg, r + dr))
    if gathers:
        depth = k1.shape[3]
        own = pl.ds(pl.multiple_of(g * depth, depth), depth)
        landings = [
            pltpu.make_async_copy(
                kernels[n // 3].at[:, n % 3], w.at[n, :, :, own, :], own_sem.at[n]
            )
            for n in range(6)
        ]
        for landing in landings:
            landing.start()
    barrier = pltpu.get_barrier_semaphore()
    total = 0
    for ok, tg, tr in greet:
        @pl.when(ok)
        def _(tg=tg, tr=tr):
            pl.semaphore_signal(barrier, inc=1, device_id=(tg, tr), device_id_type=MESH)
        total = total + ok.astype(jnp.int32)
    pl.semaphore_wait(barrier, total)

    def send(ok, src, dst, ssem, rsem, tg, tr):
        copy = pltpu.make_async_remote_copy(
            src_ref=src, dst_ref=dst, send_sem=ssem, recv_sem=rsem,
            device_id=(tg, tr), device_id_type=MESH,
        )

        @pl.when(ok)
        def _():
            copy.start()
        pending.append((ok, copy))

    if gathers:
        mine = 2 * c + (1 - c) * x

        def piece(n, t, s):
            return w.at[n, t, :, pl.ds(pl.multiple_of(s * depth, depth), depth), :]

        def piece_copy(n, t, s, way, to):
            there = piece(n, t, s)
            return pltpu.make_async_remote_copy(
                src_ref=there, dst_ref=there, send_sem=piece_send.at[n, s, way],
                recv_sem=piece_recv.at[n, t, s], device_id=(to[1], to[2]),
                device_id_type=MESH,
            )

        def send_piece(n, t, s, way, to):
            piece_copy(n, t, s, way, to).start()

        def sent_piece(n, t, s, way, to):
            piece_copy(n, t, s, way, to).wait_send()

        def wait_piece(n, t, s):
            piece_copy(n, t, s, 0, sibling).wait_recv()

        gaps = [jnp.where(z < 2, nz - o, o) for o in range(1, nz)]
        line = [(z + nz - gap) % nz * ny + y for gap in gaps]
        inner = jnp.logical_and(z > 0, z < nz - 1)
        far_end = (always, (nz - 1) * (z - 1) * ny + y, r)
        first = line + [z * ny + (1 - y)]
        second = [(z + nz - gap) % nz * ny + (1 - y) for gap in gaps]

        def own_pieces(n, act_on):
            for o in range(1, nz):
                zz = (z + o) % nz

                @pl.when(jnp.abs(zz - z) < nz - 1)
                def _(o=o, zz=zz):
                    act_on(n, mine, g, o - 1, (always, zz * ny + y, r))
                if o == 1:
                    act_on(n, mine, g, 3, across)

        def passed_on(n, group, act_on):
            for k, s in enumerate(group):
                if act_on is send_piece:
                    wait_piece(n, mine, s)
                if group is first and k == 1:
                    @pl.when(inner)
                    def _(s=s):
                        act_on(n, mine, s, 4, far_end)
                if group is first and k < nz - 1:
                    far = k == 1 if k < 2 else jnp.logical_not(inner)

                    @pl.when(jnp.logical_or(c == 0, far))
                    def _(s=s):
                        act_on(n, mine, s, 0, across)
                elif group is first:
                    @pl.when(jnp.logical_and(c == 1, z < nz - 1))
                    def _(s=s):
                        act_on(n, mine, s, 5, (always, g + ny, r))

                    @pl.when(jnp.logical_and(c == 1, z > 0))
                    def _(s=s):
                        act_on(n, mine, s, 6, (always, g - ny, r))

                @pl.when(c == 0)
                def _(s=s):
                    act_on(n, mine, s, 1, other)
                act_on(n, mine, s, 2, sibling)

        def relay(n, group):
            passed_on(n, group, send_piece)

        def cross(n, group):
            @pl.when(c == 1)
            def _():
                for s in group:
                    wait_piece(n, 1 - x, s)
                    send_piece(n, 1 - x, s, 3, sibling)

        def finish(n):
            for s in first + second:
                wait_piece(n, 2 * (1 - c) + c * x, s)

            @pl.when(c == 0)
            def _():
                for s in first + second:
                    wait_piece(n, 1 - x, s)

        def drain(n, carry):
            own_pieces(n, sent_piece)
            passed_on(n, first, sent_piece)
            passed_on(n, second, sent_piece)

            @pl.when(c == 1)
            def _():
                for s in first + second:
                    sent_piece(n, 1 - x, s, 3, sibling)
            return carry

        for landing in landings:
            landing.wait()
        own_pieces(0, send_piece)
        own_pieces(1, send_piece)

    def share_edges(i, read, gain):
        for s in range(slots):
            done = norm_act(read(s), gain[...][None, :]).reshape(rows, cols, ch)
            act[i, s] = done
            pad[i, 2 + s, 1 : 1 + rows] = done
        last[i] = act[i, pl.ds(jnp.clip(count[0] - 2, 0, slots - 2), 2)]

        @pl.when(r == 0)
        def _():
            pad[i, :, 0] = jnp.zeros((slots + 2, cols, ch), BF16)

        @pl.when(r == nr - 1)
        def _():
            pad[i, :, rows + 1] = jnp.zeros((slots + 2, cols, ch), BF16)

        @pl.when(g == 0)
        def _():
            pad[i, 0:2] = jnp.zeros((2, rows + 2, cols, ch), BF16)

        mine_in = pad.at[i]
        below, above, after = r < nr - 1, r > 0, g < ng - 1
        whole = pl.ds(2, slots)
        two = pl.ds(0, 2)
        plan = [
            (below, act.at[i, :, rows - 1], mine_in.at[whole, 0], g, r + 1, r > 0),
            (above, act.at[i, :, 0], mine_in.at[whole, rows + 1], g, r - 1, r < nr - 1),
            (after, last.at[i], mine_in.at[two, pl.ds(1, rows)], g + 1, r, g > 0),
            (
                jnp.logical_and(after, below), last.at[i, :, rows - 1],
                mine_in.at[two, 0], g + 1, r + 1, jnp.logical_and(g > 0, r > 0),
            ),
            (
                jnp.logical_and(after, above), last.at[i, :, 0],
                mine_in.at[two, rows + 1], g + 1, r - 1, jnp.logical_and(g > 0, r < nr - 1),
            ),
        ]
        waits = []
        for n, (ok, src, dst, tg, tr, comes) in enumerate(plan):
            send(ok, src, dst, halo_send.at[i, n], halo_recv.at[i, n], tg, tr)
            waits.append((comes, pending[-1][1]))
        return waits

    def gather_columns(i, waits):
        for comes, copy in waits:
            @pl.when(comes)
            def _(copy=copy):
                copy.wait_recv()
        size = (rows + 2) * cols
        col = lax.broadcasted_iota(jnp.int32, (size, ch), 0) % cols

        def body(f, carry):
            middle = pad[i, f].reshape(size, ch)
            wide = middle.astype(F32)
            left = jnp.where(col == 0, 0.0, pltpu.roll(wide, 1, 0)).astype(BF16)
            right = jnp.where(col == cols - 1, 0.0, pltpu.roll(wide, size - 1, 0)).astype(BF16)
            shape = (rows + 2, cols, ch)
            a3[f, :, :, 0:ch] = left.reshape(shape)
            a3[f, :, :, ch : 2 * ch] = middle.reshape(shape)
            a3[f, :, :, 2 * ch : 3 * ch] = right.reshape(shape)
            return carry

        lax.fori_loop(0, slots + 2, body, 0)

    def clear():
        acc[...] = jnp.zeros(acc.shape, F32)

    position = []
    for s in range(slots):
        frame = start[0] + s
        begin, end = jnp.int32(0), jnp.int32(0)
        for m in range(lengths.shape[0]):
            end = end + lengths[m]
            begin = jnp.where(end <= frame, jnp.maximum(begin, end), begin)
        position.append(frame - begin)

    def taps(i, p):
        def body(t, carry):
            lhs = a3[pl.ds(t, slots), pl.ds(p, rows)].reshape(slots * per, 3 * ch)
            held = w[3 * i + p, t] if gathers else kernels[i][t, p]
            part = jnp.dot(lhs, held.reshape(3 * ch, ch), preferred_element_type=F32)
            for s in range(slots):
                kept = jnp.where(position[s] >= 2 - t, 1.0, 0.0)
                acc[s] += part[s * per : (s + 1) * per] * kept
            return carry

        lax.fori_loop(0, 3, body, 0)

    def read_frame(s):
        return frames[s].reshape(per, ch).astype(F32)

    def tick(n, more):
        relay(n, first)
        if more:
            own_pieces(n + 2, send_piece)
        relay(n - 1, second)
        cross(n - 1, first)
        cross(n - 2, second)
        finish(n - 2)

    def early(n, carry):
        tick(n, True)
        taps(0, n - 2)
        return carry

    def all_taps(i):
        def body(p, carry):
            taps(i, p)
            return carry

        lax.fori_loop(0, 3, body, 0)

    def edges_again():
        return share_edges(1, lambda s: acc[s], gain2)

    waits = share_edges(0, read_frame, gain1)
    if gathers:
        relay(0, first)
        own_pieces(2, send_piece)
        gather_columns(0, waits)
        clear()
        relay(1, first)
        own_pieces(3, send_piece)
        relay(0, second)
        cross(0, first)
        lax.fori_loop(2, 4, early, 0)
        tick(4, False)
        taps(0, 2)
        waits = edges_again()
        tick(5, False)
        gather_columns(1, waits)
        clear()
        taps(1, 0)
        relay(5, second)
        cross(5, first)
        cross(4, second)
        finish(4)
        taps(1, 1)
        cross(5, second)
        finish(5)
        taps(1, 2)
    else:
        gather_columns(0, waits)
        clear()
        all_taps(0)
        gather_columns(1, edges_again())
        clear()
        all_taps(1)
    for s in range(slots):
        kept = jnp.where(s < count[0], read_frame(s) + acc[s], 0.0)
        out[s] = kept.astype(BF16).reshape(rows, cols, ch)
    for ok, copy in pending:
        @pl.when(ok)
        def _(copy=copy):
            copy.wait_send()
    if gathers:
        lax.fori_loop(0, 6, drain, 0)


def per_device(
    layout, frames, clip_lengths, group_start, group_count, kernel_one, kernel_two, gain_one, gain_two
):
    nz, ny, nr = layout
    slots, rows, cols, ch = frames.shape
    depth = kernel_one.shape[3]
    gathers = depth % 16 == 0 and (nz, ny, nr) == (4, 2, 4)
    if not gathers:
        kernel_one = lax.all_gather(kernel_one, "group", axis=3, tiled=True)
        kernel_two = lax.all_gather(kernel_two, "group", axis=3, tiled=True)
    vmem = pl.BlockSpec(memory_space=pltpu.VMEM)
    smem = pl.BlockSpec(memory_space=pltpu.SMEM)
    weight_spec = pl.BlockSpec(memory_space=pl.ANY) if gathers else vmem
    full = (6, 3, 3, ch, ch) if gathers else (16, 128)
    shards = lax.axis_size("group")
    dma = pltpu.SemaphoreType.DMA
    return pl.pallas_call(
        functools.partial(kernel, layout, gathers),
        out_shape=jax.ShapeDtypeStruct(frames.shape, BF16),
        in_specs=[vmem, weight_spec, weight_spec, vmem, vmem, smem, smem, smem],
        out_specs=vmem,
        scratch_shapes=[
            pltpu.VMEM(full, BF16),
            pltpu.VMEM((2, slots, rows, cols, ch), BF16),
            pltpu.VMEM((2, 2, rows, cols, ch), BF16),
            pltpu.VMEM((2, slots + 2, rows + 2, cols, ch), BF16),
            pltpu.VMEM((slots + 2, rows + 2, cols, 3 * ch), BF16),
            pltpu.VMEM((slots, rows * cols, ch), F32),
            dma((6, 3, shards) if gathers else (1,)),
            dma((6, shards, 7) if gathers else (1,)),
            dma((2, 5)),
            dma((2, 5)),
            dma((6,)),
        ],
        compiler_params=pltpu.CompilerParams(
            collective_id=0, has_side_effects=True, vmem_limit_bytes=56 * 1024 * 1024
        ),
    )(
        frames, kernel_one, kernel_two, gain_one, gain_two, clip_lengths, group_start, group_count
    )


def solution(mesh):
    groups, rows = mesh.shape["group"], mesh.shape["row"]
    ny = math.isqrt(groups // 2)
    return jax.shard_map(
        functools.partial(per_device, (groups // ny, ny, rows)),
        mesh=mesh,
        in_specs=(
            P("group", "row", None, None),
            P(),
            P("group"),
            P("group"),
            P(None, None, None, "group", None),
            P(None, None, None, "group", None),
            P(),
            P(),
        ),
        out_specs=P("group", "row", None, None),
        check_vma=False,
    )
```
